512 devices in a mesh: gx: 8 (over z_hi, core), gy: 8 (over y), gz: 8 (over z_lo, x).
Axes of the slice: x: 4, y: 8, z: 8 (z_hi: 4, z_lo: 2; z = z_hi * 2 + z_lo), core: 2. Of those that a mesh axis runs over, the one named last changes fastest.
Arguments:
- normed: bfloat16 [4096, 3072], P(('gx', 'gz'), 'gy'), may hold values from -6 to 6
- grad_out: bfloat16 [4096, 3072], P(('gx', 'gz'), 'gy'), may hold values from -0.75 to 0.75
- grad_qkv_out: bfloat16 [4096, 9216], P(('gx', 'gy'), 'gz'), may hold values from -0.75 to 0.75
- pre_act: bfloat16 [4096, 12288], P(('gx', 'gy'), 'gz'), may hold values from -9 to 9
- w_qkv: bfloat16 [3072, 9216], P(('gy', 'gx'), 'gz'), may hold values from -0.109375 to 0.109375
- w_up: bfloat16 [3072, 12288], P(('gy', 'gx'), 'gz'), may hold values from -0.109375 to 0.109375
- w_down: bfloat16 [12288, 3072], P(('gz', 'gx'), 'gy'), may hold values from -0.0546875 to 0.0546875
Outputs:
- grad_input: bfloat16 [4096, 3072], P(('gx', 'gz'), 'gy')
- grad_w_qkv: bfloat16 [3072, 9216], P(('gy', 'gx'), 'gz')
- grad_w_up: bfloat16 [3072, 12288], P(('gy', 'gx'), 'gz')
- grad_w_down: bfloat16 [12288, 3072], P(('gz', 'gx'), 'gy')
The draws below stay inside these ranges and needn't reach their ends.
All inputs are finite; a program needn't handle non-finite values.
Results may differ from the reference program's by a relative error of at most 0.028.
Values may be sent and summed in bfloat16 or wider, within the bound.
A program may use at most 64 MiB of HBM per device.

```python
import jax
import jax.numpy as jnp
from jax import lax

D = 3072
FF = 12288
QKV = 9216
TOKENS = 4096
N_GX = 8


def level_of(stream_key, dims, split, smallest, top_value):
    def one(position, parts):
        draws = jax.random.uniform(jax.random.fold_in(jax.random.fold_in(stream_key, 6), position), (parts,), jnp.float32, smallest / len(split), top_value / len(split))
        return jnp.repeat(jnp.exp(draws), dims[position] // parts).reshape((-1,) + (1,) * (len(dims) - position - 1))

    loudness = one(*split[0])
    for cut in split[1:]:
        loudness = loudness * one(*cut)
    return loudness


def normal_values(rng, extent, width, most, pieces=(), held_as=jnp.bfloat16):
    values = jax.random.normal(rng, extent, jnp.float32) * width
    if len(pieces) > 0:
        values = level_of(rng, extent, pieces, -0.22, 0.18) * values
    return jnp.clip(values, min=-most, max=most).astype(held_as)


def setup_inputs(seed: int = 0) -> dict:
    key_of = jax.random.split(jax.random.key(seed), 8)
    normed = normal_values(key_of[0], (TOKENS, D), 1.0, 6.0, ((0, 64), (1, 8)))
    grad_out = normal_values(key_of[1], (TOKENS, D), 0.125, 0.75, ((0, 64), (1, 8)))
    grad_qkv_out = normal_values(key_of[2], (TOKENS, QKV), 0.125, 0.75, ((0, 64), (1, 8)))
    pre_act = normal_values(key_of[3], (TOKENS, FF), 1.5, 9.0, ((0, 64), (1, 8)))
    w_qkv = normal_values(key_of[4], (D, QKV), D ** -0.5, 0.109375, ((0, 64), (1, 8)))
    w_up = normal_values(key_of[5], (D, FF), D ** -0.5, 0.109375, ((0, 64), (1, 8)))
    w_down = normal_values(key_of[6], (FF, D), FF ** -0.5, 0.0546875, ((0, 64), (1, 8)))
    return {"normed": normed, "grad_out": grad_out, "grad_qkv_out": grad_qkv_out, "pre_act": pre_act, "w_qkv": w_qkv, "w_up": w_up, "w_down": w_down}


def gelu_parts(pre_act):
    pre_float = pre_act.astype(jnp.float32)
    normal_cdf = 0.5 * (1.0 + lax.erf(pre_float * 0.7071067811865476))
    normal_pdf = jnp.exp(-0.5 * pre_float * pre_float) * 0.3989422804014327
    return (pre_float * normal_cdf, normal_cdf + pre_float * normal_pdf)

def blocked_grad(left, right):
    left_blocks = left.reshape(N_GX, -1, left.shape[1])
    right_blocks = right.reshape(N_GX, -1, right.shape[1])

    def add_block(total, pair):
        product = jnp.dot(pair[0].T, pair[1], preferred_element_type=jnp.float32)
        rounded = lax.optimization_barrier(product.astype(jnp.bfloat16))
        return (total + rounded.astype(jnp.float32), None)
    initial = jnp.zeros((left.shape[1], right.shape[1]), jnp.float32)
    total, ignored = lax.scan(add_block, initial, (left_blocks, right_blocks))
    return total.astype(jnp.bfloat16)

def reference(normed, grad_out, grad_qkv_out, pre_act, w_qkv, w_up, w_down):
    gelu_value, gelu_slope = gelu_parts(pre_act)
    activated = gelu_value.astype(jnp.bfloat16)
    grad_act = jnp.dot(grad_out, w_down.T, preferred_element_type=jnp.float32)
    grad_pre = (grad_act * gelu_slope).astype(jnp.bfloat16)
    grad_w_down = blocked_grad(activated, grad_out)
    grad_w_qkv = blocked_grad(normed, grad_qkv_out)
    grad_w_up = blocked_grad(normed, grad_pre)
    summed = jnp.dot(grad_qkv_out, w_qkv.T, preferred_element_type=jnp.float32)
    summed = summed + jnp.dot(grad_pre, w_up.T, preferred_element_type=jnp.float32)
    return (summed.astype(jnp.bfloat16), grad_w_qkv, grad_w_up, grad_w_down)
```

```python
import jax
import jax.numpy as jnp
from jax import lax
from jax.experimental import pallas as pl
from jax.experimental.pallas import tpu as pltpu
from jax.sharding import PartitionSpec as P

MESH = pl.DeviceIdType.MESH
BF = jnp.bfloat16
F32 = jnp.float32
N = 8
ROWS = 64
DM = 384
QW = 1152
FW = 1536
CH = 768
QA = 640
QB = 512
COPIES = 160


def dot_bt(a, b):
    return lax.dot_general(a, b, (((1,), (1,)), ((), ())), preferred_element_type=F32)


def dot_ta(a, b):
    return lax.dot_general(a, b, (((0,), (0,)), ((), ())), preferred_element_type=F32)


def dot(a, b):
    return jnp.dot(a, b, preferred_element_type=F32)


def wrap(i):
    return lax.rem(i + 2 * N, N)


def rows_of(slot, size, start=0, count=None):
    count = size if count is None else count
    return pl.ds(pl.multiple_of(slot * size + start, 16), count)


def kernel(
    n_in, g_in, q_in, p_in, wq_in, wu_in, wd_in,
    gi_out, gwq_out, gwu_out, gwd_out,
    normed, normed_t, grads, qkv, act, slope, w_down, w_up, w_qkv,
    part, part_r, part_l, gpre, summed, outgoing, in_x, in_z,
    d_part, d_sib, d_first, d_last,
    ua_part, ua_sib, ua_first, ua_last,
    ub_part, ub_sib, ub_first, ub_last,
    qa_part, qa_sib, qa_first, qa_last,
    qb_part, qb_sib, qb_first, qb_last,
    send_sems, recv_sems,
):
    gx, gy, gz = lax.axis_index("gx"), lax.axis_index("gy"), lax.axis_index("gz")
    core = lax.rem(gx, 2)
    chip = gx // 2
    z_lo, x = gz // 4, lax.rem(gz, 4)

    sib = (gx + 1 - 2 * core, gy, gz)
    chip_r, chip_l = (wrap(gx + 2), gy, gz), (wrap(gx - 2), gy, gz)
    up, down = (gx, wrap(gy + 1), gz), (gx, wrap(gy - 1), gz)
    zp = (gx, gy, wrap(gz + 4))

    def x_index(shift):
        return lax.rem(x + shift, 4)

    xs = [(gx, gy, z_lo * 4 + x_index(d)) for d in (1, 2, 3)]

    barrier = pltpu.get_barrier_semaphore()
    peers = [sib, chip_r, chip_l, up, down, zp] + xs
    for peer in peers:
        pl.semaphore_signal(barrier, inc=1, device_id=peer, device_id_type=MESH)

    started = []

    def send(src, dst, peer):
        i = len(started)
        copy = pltpu.make_async_remote_copy(
            src_ref=src, dst_ref=dst, send_sem=send_sems.at[i], recv_sem=recv_sems.at[i],
            device_id=peer, device_id_type=MESH,
        )
        copy.start()
        started.append(copy)
        return copy

    class ChipGather:
        def __init__(self, own, full, size):
            self.own, self.full, self.size = own, full, size

        def at(self, shift):
            return self.full.at[rows_of(wrap(gx + shift), self.size)]

        def half(self, shift, h):
            slot = wrap(gx + shift)
            if self.size % 32 == 0:
                return self.full.at[rows_of(slot, self.size, h * self.size // 2, self.size // 2)]
            width = self.full.shape[1] // 256 * 128
            cols = pl.ds(0, width) if h == 0 else pl.ds(width, self.full.shape[1] - width)
            return self.full.at[rows_of(slot, self.size), cols]

        def start(self):
            me = self.at(0)
            self.to_sib = [send(self.own, me, sib)]
            self.to_r = send(self.own, me, chip_r)
            self.to_l = send(self.own, me, chip_l)
            self.full[rows_of(gx, self.size)] = self.own[...]

        def forward(self):
            self.to_r.wait_recv()
            self.far_r = send(self.half(-2, 0), self.half(-2, 0), chip_r)
            self.to_l.wait_recv()
            self.far_l = send(self.half(2, 1), self.half(2, 1), chip_l)
            self.to_sib.append(send(self.at(-2), self.at(-2), sib))
            self.to_sib.append(send(self.at(2), self.at(2), sib))

        def finish(self):
            self.far_r.wait_recv()
            self.to_sib.append(send(self.half(4, 0), self.half(4, 0), sib))
            self.far_l.wait_recv()
            self.to_sib.append(send(self.half(4, 1), self.half(4, 1), sib))

        def complete(self):
            for copy in self.to_sib:
                copy.wait_recv()

    class RingGather:
        def __init__(self, full):
            self.full = full

        def at(self, shift, start=0, count=ROWS):
            return self.full.at[rows_of(wrap(gy + shift), ROWS, start, count)]

        def start(self):
            self.step = 0
            self.go_up = send(self.at(0), self.at(0), up)
            self.go_down = send(self.at(0), self.at(0), down)

        def forward(self):
            self.step += 1
            s = self.step
            start_up, start_down, count = (0, 0, ROWS) if s < 3 else (0, ROWS // 2, ROWS // 2)
            self.go_up.wait_recv()
            if s < 4:
                src = self.at(-s, start_up, count)
                self.go_up = send(src, src, up)
            self.go_down.wait_recv()
            if s < 4:
                src = self.at(s, start_down, count)
                self.go_down = send(src, src, down)

    class RingReduce:
        def __init__(self, c):
            self.c = c
            self.mine = part.at[c]

        def at(self, shift, start=0, count=ROWS):
            return rows_of(wrap(gy + shift), ROWS, start, count)

        def start(self):
            half = ROWS // 2
            self.step = 1
            self.go_up = send(self.mine.at[self.at(4, 0, half)], part_r.at[self.c, 0, pl.ds(0, half)], up)
            self.go_down = send(self.mine.at[self.at(4, half, half)], part_l.at[self.c, 0, pl.ds(half, half)], down)

        def add(self, rows, other):
            self.mine[rows] = (self.mine[rows].astype(F32) + other.astype(F32)).astype(BF)

        def forward(self):
            s = self.step
            half = ROWS // 2
            self.go_up.wait_recv()
            if s == 1:
                self.add(self.at(3, 0, half), part_r[self.c, 0, 0:half])
            else:
                self.add(self.at(4 - s), part_r[self.c, s - 1])
            self.go_up = send(self.mine.at[self.at(4 - s)], part_r.at[self.c, s], up)
            self.go_down.wait_recv()
            if s == 1:
                self.add(self.at(-3, half, half), part_l[self.c, 0, half:ROWS])
            else:
                self.add(self.at(s - 4), part_l[self.c, s - 1])
            self.go_down = send(self.mine.at[self.at(s - 4)], part_l.at[self.c, s], down)
            self.step += 1

        def finish(self):
            self.go_up.wait_recv()
            self.go_down.wait_recv()
            c = self.c

            def body(i, carry):
                r = pl.ds(pl.multiple_of(i * 16, 16), 16)
                rows = rows_of(gy, ROWS, i * 16, 16)
                total = self.mine[rows].astype(F32) + part_r[c, 3, r].astype(F32) + part_l[c, 3, r].astype(F32)
                gpre[c, rows] = (total * slope[r, CH * c : CH * c + CH]).astype(BF)
                return carry

            lax.fori_loop(0, ROWS // 16, body, 0)

    class PlaneGather:
        def __init__(self, own, full):
            self.own, self.full = own, full

        def at(self, shift):
            return self.full.at[rows_of(wrap(gz + shift), ROWS)]

        def start(self):
            self.to_z = send(self.own, self.at(0), zp)
            self.to_x = [send(self.own, self.at(0), peer) for peer in xs]
            self.full[rows_of(gz, ROWS)] = self.own[...]

        def forward(self):
            self.to_z.wait_recv()
            self.to_x += [send(self.at(4), self.at(4), peer) for peer in xs]

        def complete(self):
            for copy in self.to_x:
                copy.wait_recv()

    class ChipReduce:
        def __init__(self, halves):
            self.halves = halves

        def start(self):
            self.swap = [send(p.at[1 - core], s, sib) for p, s, _, _ in self.halves]

        def total(self, h, k):
            p, s, _, _ = self.halves[h]
            return p[core, k].astype(F32) + s[k].astype(F32)

        def put(self, h, k, value):
            self.halves[h][0][core, k] = value.astype(BF)

        def chips(self):
            for copy in self.swap:
                copy.wait_recv()
            far, right, left = (lax.rem(chip + i, 4) for i in (2, 1, 3))
            (pa, _, fa, la), (pb, _, fb, lb) = self.halves
            self.put(0, far, self.total(0, far))
            self.far_r = send(pa.at[core, far], fa, chip_r)
            self.put(1, far, self.total(1, far))
            self.far_l = send(pb.at[core, far], fb, chip_l)
            self.put(1, right, self.total(1, right))
            self.near = [send(pb.at[core, right], lb.at[0], chip_r)]
            self.put(0, left, self.total(0, left))
            self.near.append(send(pa.at[core, left], la.at[1], chip_l))

        def forward(self):
            right, left = (lax.rem(chip + i, 4) for i in (1, 3))
            (pa, _, fa, la), (pb, _, fb, lb) = self.halves
            self.far_r.wait_recv()
            self.put(0, right, self.total(0, right) + fa[...].astype(F32))
            self.near.append(send(pa.at[core, right], la.at[0], chip_r))
            self.far_l.wait_recv()
            self.put(1, left, self.total(1, left) + fb[...].astype(F32))
            self.near.append(send(pb.at[core, left], lb.at[1], chip_l))

        def finish(self, store):
            for copy in self.near:
                copy.wait_recv()
            for h in (0, 1):
                last = self.halves[h][3]
                store(h, (self.total(h, chip) + last[0].astype(F32) + last[1].astype(F32)).astype(BF))

    def gelu():
        def body(i, carry):
            r = pl.ds(pl.multiple_of(i * 16, 16), 16)
            for c in range(0, FW, DM):
                v = p_in[r, c : c + DM].astype(F32)
                cdf = 0.5 * (1.0 + lax.erf(v * 0.7071067811865476))
                pdf = jnp.exp(-0.5 * v * v) * 0.3989422804014327
                act[rows_of(gy, ROWS, i * 16, 16), c : c + DM] = (v * cdf).astype(BF)
                slope[r, c : c + DM] = cdf + v * pdf
            return carry

        lax.fori_loop(0, ROWS // 16, body, 0)

    def partial_act(c):
        def body(i, carry):
            r = pl.ds(pl.multiple_of(i * 256, 256), 256)
            part[c, r] = dot_bt(grads[r], w_down[c * CH : c * CH + CH]).astype(BF)
            return carry

        lax.fori_loop(0, 2, body, 0)

    def grad_down():
        def body(k, carry):
            cols = pl.ds(pl.multiple_of(k * DM, DM), DM)
            product = dot_ta(act[:, cols], grads[...]).astype(BF)
            for c in (0, 1):
                for h in (0, 1):
                    at = 192 * c + 96 * h
                    d_part[h, c, k] = product[at : at + 96]
            return carry

        lax.fori_loop(0, 4, body, 0)

    def split(product, target):
        for g in range(N):
            target[g % 2, g // 2] = product[48 * g : 48 * g + 48]

    def grad_qkv():
        split(dot(normed_t[...], qkv[:, 0:QA]).astype(BF), qa_part)
        split(dot(normed_t[...], qkv[:, QA:QW]).astype(BF), qb_part)

    def grad_up(c):
        target = (ua_part, ub_part)[c]
        for h in (0, 1):
            split(dot(normed_t[...], gpre[c, :, h * DM : h * DM + DM]).astype(BF), target.at[h])

    def input_qkv():
        def body(i, carry):
            r = pl.ds(pl.multiple_of(i * 256, 256), 256)
            summed[r] = dot_bt(qkv[r], w_qkv[...])
            return carry

        lax.fori_loop(0, 2, body, 0)

    def input_up():
        def body(i, carry):
            r = pl.ds(pl.multiple_of(i * 256, 256), 256)
            total = summed[r]
            for c in (0, 1):
                total = total + dot_bt(gpre[c, r], w_up[:, c * CH : c * CH + CH])
            outgoing[r] = total.astype(BF)
            return carry

        lax.fori_loop(0, 2, body, 0)

    plane = {}

    def plane_start():
        plane["x"] = [
            send(outgoing.at[rows_of(z * 4 + x_index(d), ROWS)], in_x.at[d - 1, z], xs[d - 1])
            for d in (1, 2, 3)
            for z in (0, 1)
        ]

    def plane_total(z):
        total = outgoing[rows_of(z * 4 + x, ROWS)].astype(F32)
        for d in range(3):
            total = total + in_x[d, z].astype(F32)
        return total

    def plane_forward():
        for copy in plane["x"]:
            copy.wait_recv()
        rows = rows_of((1 - z_lo) * 4 + x, ROWS)
        outgoing[rows] = plane_total(1 - z_lo).astype(BF)
        plane["z"] = send(outgoing.at[rows], in_z, zp)

    def plane_finish():
        plane["z"].wait_recv()
        gi_out[...] = (plane_total(z_lo) + in_z[...].astype(F32)).astype(BF)

    def store_down(h, value):
        gwd_out[96 * h : 96 * h + 96] = value

    def store_qkv(h, value):
        cols = slice(0, QA) if h == 0 else slice(QA, QW)
        gwq_out[:, cols] = value

    def store_up(c):
        def store(h, value):
            at = c * CH + h * DM
            gwu_out[:, at : at + DM] = value

        return store

    wd, wu, wq = ChipGather(wd_in, w_down, 192), ChipGather(wu_in, w_up, 48), ChipGather(wq_in, w_qkv, 48)
    ga, gq, gp = RingGather(act), RingGather(qkv), [RingGather(gpre.at[c]) for c in (0, 1)]
    rr = [RingReduce(c) for c in (0, 1)]
    pg, pn = PlaneGather(g_in, grads), PlaneGather(n_in, normed)
    rd = ChipReduce([(d_part.at[h], d_sib.at[h], d_first.at[h], d_last.at[h]) for h in (0, 1)])
    ru = [
        ChipReduce([(p.at[h], s.at[h], f.at[h], t.at[h]) for h in (0, 1)])
        for p, s, f, t in ((ua_part, ua_sib, ua_first, ua_last), (ub_part, ub_sib, ub_first, ub_last))
    ]
    rq = ChipReduce([(qa_part, qa_sib, qa_first, qa_last), (qb_part, qb_sib, qb_first, qb_last)])

    qkv[rows_of(gy, ROWS)] = q_in[...]
    gelu()
    pl.semaphore_wait(barrier, len(peers))

    pg.start()
    wd.start()
    ga.start()
    gq.start()
    pn.start()
    pg.forward()
    pn.forward()
    ga.forward()
    wd.forward()
    wu.start()
    gq.forward()
    pg.complete()
    ga.forward()
    wd.finish()
    wd.complete()
    partial_act(0)
    rr[0].start()
    partial_act(1)
    rr[1].start()
    gq.forward()
    wu.forward()
    wq.start()
    pn.complete()
    normed_t[...] = normed[...].T
    rr[0].forward()
    rr[1].forward()
    ga.forward()
    wu.finish()
    rr[0].forward()
    rr[1].forward()
    gq.forward()
    wq.forward()
    ga.forward()
    rr[0].forward()
    rr[1].forward()
    grad_down()
    rd.start()
    rr[0].finish()
    gp[0].start()
    rr[1].finish()
    gp[1].start()
    rd.chips()
    wq.finish()
    gq.forward()
    gp[0].forward()
    gp[1].forward()
    grad_qkv()
    rq.start()
    rd.forward()
    gp[0].forward()
    gp[1].forward()
    rq.chips()
    wq.complete()
    input_qkv()
    rd.finish(store_down)
    gp[0].forward()
    gp[1].forward()
    rq.forward()
    wu.complete()
    gp[0].forward()
    grad_up(0)
    ru[0].start()
    gp[1].forward()
    grad_up(1)
    ru[1].start()
    ru[0].chips()
    input_up()
    plane_start()
    ru[1].chips()
    rq.finish(store_qkv)
    ru[0].forward()
    ru[1].forward()
    plane_forward()
    ru[0].finish(store_up(0))
    plane_finish()
    ru[1].finish(store_up(1))
    for copy in started:
        copy.wait_send()


def reduce_scratch(rows, width, halves=None):
    lead = () if halves is None else (halves,)
    return [
        pltpu.VMEM(lead + (2, 4, rows, width), BF),
        pltpu.VMEM(lead + (4, rows, width), BF),
        pltpu.VMEM(lead + (rows, width), BF),
        pltpu.VMEM(lead + (2, rows, width), BF),
    ]


def shards(normed, grad_out, grad_qkv_out, pre_act, w_qkv, w_up, w_down):
    outs = (normed, w_qkv, w_up, w_down)
    return pl.pallas_call(
        kernel,
        out_shape=[jax.ShapeDtypeStruct(o.shape, BF) for o in outs],
        in_specs=[pl.BlockSpec(memory_space=pltpu.VMEM)] * 7,
        out_specs=[pl.BlockSpec(memory_space=pltpu.VMEM)] * 4,
        scratch_shapes=[
            pltpu.VMEM((N * ROWS, DM), BF),
            pltpu.VMEM((DM, N * ROWS), BF),
            pltpu.VMEM((N * ROWS, DM), BF),
            pltpu.VMEM((N * ROWS, QW), BF),
            pltpu.VMEM((N * ROWS, FW), BF),
            pltpu.VMEM((ROWS, FW), F32),
            pltpu.VMEM((FW, DM), BF),
            pltpu.VMEM((DM, FW), BF),
            pltpu.VMEM((DM, QW), BF),
            pltpu.VMEM((2, N * ROWS, CH), BF),
            pltpu.VMEM((2, 4, ROWS, CH), BF),
            pltpu.VMEM((2, 4, ROWS, CH), BF),
            pltpu.VMEM((2, N * ROWS, CH), BF),
            pltpu.VMEM((N * ROWS, DM), F32),
            pltpu.VMEM((N * ROWS, DM), BF),
            pltpu.VMEM((3, 2, ROWS, DM), BF),
            pltpu.VMEM((ROWS, DM), BF),
            *reduce_scratch(96, DM, 2),
            *reduce_scratch(48, DM, 2),
            *reduce_scratch(48, DM, 2),
            *reduce_scratch(48, QA),
            *reduce_scratch(48, QB),
            pltpu.SemaphoreType.DMA((COPIES,)),
            pltpu.SemaphoreType.DMA((COPIES,)),
        ],
        compiler_params=pltpu.CompilerParams(
            collective_id=0, has_side_effects=True, vmem_limit_bytes=48 << 20
        ),
    )(normed, grad_out, grad_qkv_out, pre_act, w_qkv, w_up, w_down)


def solution(mesh):
    rows, tall = P(("gx", "gz"), "gy"), P(("gx", "gy"), "gz")
    block, flat = P(("gy", "gx"), "gz"), P(("gz", "gx"), "gy")
    return jax.shard_map(
        shards,
        mesh=mesh,
        in_specs=(rows, rows, tall, tall, block, block, flat),
        out_specs=(rows, block, block, flat),
        check_vma=False,
    )
```

```python
import jax
import jax.numpy as jnp
from jax import lax
from jax.experimental import pallas as pl
from jax.experimental.pallas import tpu as pltpu
from jax.sharding import PartitionSpec as P

MESH = pl.DeviceIdType.MESH
BF = jnp.bfloat16
F32 = jnp.float32
N = 8
ROWS = 64
HALF = 32
DM = 384
QW = 1152
FW = 1536
QA = 640
QB = 512
WIDE = 256
COPIES = 200


def dot_bt(a, b):
    return lax.dot_general(a, b, (((1,), (1,)), ((), ())), preferred_element_type=F32)


def dot_ta(a, b):
    return lax.dot_general(a, b, (((0,), (0,)), ((), ())), preferred_element_type=F32)


def dot(a, b):
    return jnp.dot(a, b, preferred_element_type=F32)


def wrap(i):
    return lax.rem(i + 2 * N, N)


def rows_of(slot, size, start=0, count=None):
    count = size if count is None else count
    return pl.ds(pl.multiple_of(slot * size + start, 16), count)


def kernel(
    n_in, g_in, q_in, p_in, wq_in, wu_in, wd_in,
    gi_hbm, gwq_hbm, gwu_hbm, gwd_hbm,
    normed, normed_t, grads, qkv, act, slope, w_down, w_up, w_qkv,
    part, part_u, part_d, gpre, summed, outgoing, in_x, in_z,
    d_part, d_sib, d_first, d_last,
    uw_part, uw_sib, uw_first, uw_last,
    un_part, un_sib, un_first, un_last,
    qa_part, qa_sib, qa_first, qa_last,
    qb_part, qb_sib, qb_first, qb_last,
    pre, gi_out, gwq_out, gwu_out, gwd_out, send_sems, recv_sems, load_sems,
):
    gx, gy, gz = lax.axis_index("gx"), lax.axis_index("gy"), lax.axis_index("gz")
    core = lax.rem(gx, 2)
    chip = gx // 2
    z_lo, x = gz // 4, lax.rem(gz, 4)

    sib = (gx + 1 - 2 * core, gy, gz)
    chip_r, chip_l = (wrap(gx + 2), gy, gz), (wrap(gx - 2), gy, gz)
    up, down = (gx, wrap(gy + 1), gz), (gx, wrap(gy - 1), gz)
    zp = (gx, gy, wrap(gz + 4))

    def x_index(shift):
        return lax.rem(x + shift, 4)

    xs = [(gx, gy, z_lo * 4 + x_index(d)) for d in (1, 2, 3)]

    barrier = pltpu.get_barrier_semaphore()
    peers = [sib, chip_r, chip_l, up, down, zp] + xs
    for peer in peers:
        pl.semaphore_signal(barrier, inc=1, device_id=peer, device_id_type=MESH)

    loads = []

    def load(src, dst):
        copy = pltpu.make_async_copy(src, dst, load_sems.at[len(loads)])
        copy.start()
        loads.append(copy)
        return copy

    started = []

    class Send:
        def __init__(self, src, dst, peer):
            i = len(started)
            self.copy = pltpu.make_async_remote_copy(
                src_ref=src, dst_ref=dst, send_sem=send_sems.at[i], recv_sem=recv_sems.at[i],
                device_id=peer, device_id_type=MESH,
            )
            self.arrived = False
            self.copy.start()
            started.append(self)

        def wait(self):
            if not self.arrived:
                self.copy.wait_recv()
            self.arrived = True

    def wait_all(copies):
        for copy in copies:
            copy.wait()

    class ChipGather:
        def __init__(self, own, full, size, pieces):
            self.own, self.full, self.size, self.pieces = own, full, size, pieces
            self.to_sib = {}

        def half_at(self, h):
            if self.size % 32 == 0:
                return (pl.ds(h * self.size // 2, self.size // 2),)
            width = self.full.shape[1] // 256 * 128
            return (slice(None), pl.ds(0, width) if h == 0 else pl.ds(width, self.full.shape[1] - width))

        def at(self, shift):
            return self.full.at[rows_of(wrap(gx + shift), self.size)]

        def half(self, shift, h):
            return self.at(shift).at[self.half_at(h)]

        def start(self):
            if self.pieces:
                self.r, self.l = [None, None], [None, None]
                for h in (0, 1):
                    self.r[h] = Send(self.own.at[self.half_at(h)], self.half(0, h), chip_r)
                    self.l[1 - h] = Send(self.own.at[self.half_at(1 - h)], self.half(0, 1 - h), chip_l)
            else:
                self.r = [Send(self.own, self.at(0), chip_r)]
                self.l = [Send(self.own, self.at(0), chip_l)]
            self.to_sib["own"] = Send(self.own, self.at(0), sib)

        def fwd_r(self):
            self.r[0].wait()
            self.far_up = Send(self.half(-2, 0), self.half(-2, 0), chip_r)
            if not self.pieces:
                self.sh_r()

        def fwd_l(self):
            self.l[-1].wait()
            self.far_down = Send(self.half(2, 1), self.half(2, 1), chip_l)
            if not self.pieces:
                self.sh_l()

        def sh_r(self):
            wait_all(self.r)
            self.to_sib["r"] = Send(self.at(-2), self.at(-2), sib)

        def sh_l(self):
            wait_all(self.l)
            self.to_sib["l"] = Send(self.at(2), self.at(2), sib)

        def far_r(self):
            self.far_up.wait()
            self.to_sib["far_r"] = Send(self.half(4, 0), self.half(4, 0), sib)

        def far_l(self):
            self.far_down.wait()
            self.to_sib["far_l"] = Send(self.half(4, 1), self.half(4, 1), sib)

        def complete(self):
            for key in self.to_sib:
                self.to_sib[key].wait()

    class RingGather:
        def __init__(self, full, own=None):
            self.full, self.own = full, own
            self.chain = {}
            self.hops = {}

        def at(self, shift, h):
            return self.full.at[rows_of(wrap(gy + shift), ROWS, HALF * h, HALF)]

        def go(self, d, h):
            s = self.hops.get((d, h), 0)
            self.hops[d, h] = s + 1
            if s > 0:
                self.chain[d, h].wait()
            here = self.at(s if d else -s, h)
            src = self.own.at[pl.ds(HALF * h, HALF)] if s == 0 and self.own is not None else here
            self.chain[d, h] = Send(src, here, down if d else up)

        def complete(self):
            assert self.hops == {(0, 0): 4, (1, 1): 4, (0, 1): 3, (1, 0): 3}
            for key in self.chain:
                self.chain[key].wait()

    class BlockGather:
        def __init__(self, full):
            self.full = full

        def at(self, shift, start=0, count=ROWS):
            return self.full.at[rows_of(wrap(gy + shift), ROWS, start, count)]

        def start(self):
            self.step_u = self.step_d = 0
            self.to_u = Send(self.at(0), self.at(0), up)
            self.to_d = Send(self.at(0), self.at(0), down)

        def up(self):
            self.step_u += 1
            self.to_u.wait()
            src = self.at(-self.step_u, 0, ROWS if self.step_u < 3 else HALF)
            self.to_u = Send(src, src, up)

        def down(self):
            self.step_d += 1
            self.to_d.wait()
            src = self.at(self.step_d) if self.step_d < 3 else self.at(3, HALF, HALF)
            self.to_d = Send(src, src, down)

        def complete(self):
            assert self.step_u == self.step_d == 3
            self.to_u.wait()
            self.to_d.wait()

    class RingReduce:
        def __init__(self, rel):
            self.rel = rel
            self.block = lax.rem(chip + (0, 1, 3, 2)[rel], 4)
            self.mine = part.at[self.block]

        def at(self, shift, start=0, count=ROWS):
            return rows_of(wrap(gy + shift), ROWS, start, count)

        def start(self):
            pg.complete()
            if self.rel == 0:
                wd.to_sib["own"].wait()
            elif self.rel == 1:
                wait_all(wd.l + [wd.to_sib["l"]])
            elif self.rel == 2:
                wait_all(wd.r + [wd.to_sib["r"]])
            else:
                wait_all([wd.far_up, wd.far_down, wd.to_sib["far_r"], wd.to_sib["far_l"]])
            rows = rows_of(self.block, DM)

            def body(i, carry):
                r = pl.ds(pl.multiple_of(i * 256, 256), 256)
                self.mine[r] = dot_bt(grads[r], w_down[rows]).astype(BF)
                return carry

            lax.fori_loop(0, 2, body, 0)
            self.step_u = self.step_d = 1
            first = pl.ds(0, HALF), pl.ds(HALF, HALF)
            self.to_u = Send(self.mine.at[self.at(4, 0, HALF)], part_u.at[self.rel, 0, first[0]], up)
            self.to_d = Send(self.mine.at[self.at(4, HALF, HALF)], part_d.at[self.rel, 0, first[1]], down)

        def add(self, rows, other):
            self.mine[rows] = (self.mine[rows].astype(F32) + other.astype(F32)).astype(BF)

        def up(self):
            s = self.step_u
            self.step_u += 1
            self.to_u.wait()
            if s == 1:
                self.add(self.at(3, 0, HALF), part_u[self.rel, 0, 0:HALF])
            else:
                self.add(self.at(4 - s), part_u[self.rel, s - 1])
            self.to_u = Send(self.mine.at[self.at(4 - s)], part_u.at[self.rel, s], up)

        def down(self):
            s = self.step_d
            self.step_d += 1
            self.to_d.wait()
            if s == 1:
                self.add(self.at(-3, HALF, HALF), part_d[self.rel, 0, HALF:ROWS])
            else:
                self.add(self.at(s - 4), part_d[self.rel, s - 1])
            self.to_d = Send(self.mine.at[self.at(s - 4)], part_d.at[self.rel, s], down)

        def finish(self):
            assert self.step_u == self.step_d == 4
            self.to_u.wait()
            self.to_d.wait()
            rows = self.at(0)
            total = self.mine[rows].astype(F32) + part_u[self.rel, 3].astype(F32) + part_d[self.rel, 3].astype(F32)
            gpre[self.block, rows] = (total * slope[self.block]).astype(BF)

    class PlaneGather:
        def __init__(self, own, full):
            self.own, self.full = own, full

        def at(self, shift):
            return self.full.at[rows_of(wrap(gz + shift), ROWS)]

        def start(self):
            self.to_z = Send(self.own, self.at(0), zp)
            self.to_x = [Send(self.own, self.at(0), peer) for peer in xs]

        def forward(self):
            self.to_z.wait()
            self.to_x += [Send(self.at(4), self.at(4), peer) for peer in xs]

        def complete(self):
            wait_all(self.to_x)

    class ChipReduce:
        def __init__(self, halves, compute, store):
            self.halves, self.compute, self.store = halves, compute, store

        def start(self):
            self.compute()
            self.swap = [Send(p.at[1 - core], s, sib) for p, s, _, _ in self.halves]

        def total(self, h, k):
            p, s, _, _ = self.halves[h]
            return p[core, k].astype(F32) + s[k].astype(F32)

        def put(self, h, k, value):
            self.halves[h][0][core, k] = value.astype(BF)

        def chips(self):
            wait_all(self.swap)
            far, right, left = (lax.rem(chip + i, 4) for i in (2, 1, 3))
            (pa, _, fa, la), (pb, _, fb, lb) = self.halves
            self.put(0, far, self.total(0, far))
            self.far_up = Send(pa.at[core, far], fa, chip_r)
            self.put(1, far, self.total(1, far))
            self.far_down = Send(pb.at[core, far], fb, chip_l)
            self.put(1, right, self.total(1, right))
            self.near = [Send(pb.at[core, right], lb.at[0], chip_r)]
            self.put(0, left, self.total(0, left))
            self.near.append(Send(pa.at[core, left], la.at[1], chip_l))

        def fwd_r(self):
            right = lax.rem(chip + 1, 4)
            pa, _, fa, la = self.halves[0]
            self.far_up.wait()
            self.put(0, right, self.total(0, right) + fa[...].astype(F32))
            self.near.append(Send(pa.at[core, right], la.at[0], chip_r))

        def fwd_l(self):
            left = lax.rem(chip + 3, 4)
            pb, _, fb, lb = self.halves[1]
            self.far_down.wait()
            self.put(1, left, self.total(1, left) + fb[...].astype(F32))
            self.near.append(Send(pb.at[core, left], lb.at[1], chip_l))

        def finish(self):
            wait_all(self.near)
            for h in (0, 1):
                last = self.halves[h][3]
                self.store(h, (self.total(h, chip) + last[0].astype(F32) + last[1].astype(F32)).astype(BF))

    def gelu():
        def body(i, carry):
            r = pl.ds(pl.multiple_of(i * 16, 16), 16)
            for b in range(4):
                cols = slice(b * DM, b * DM + DM)
                v = pre[r, cols].astype(F32)
                cdf = 0.5 * (1.0 + lax.erf(v * 0.7071067811865476))
                pdf = jnp.exp(-0.5 * v * v) * 0.3989422804014327
                act[rows_of(gy, ROWS, i * 16, 16), cols] = (v * cdf).astype(BF)
                slope[b, r] = cdf + v * pdf
            return carry

        lax.fori_loop(0, ROWS // 16, body, 0)

    def tn():
        pn.complete()
        normed_t[...] = normed[...].T

    def grad_down():
        ga.complete()
        pg.complete()

        def body(k, carry):
            cols = pl.ds(pl.multiple_of(k * DM, DM), DM)
            product = dot_ta(act[:, cols], grads[...]).astype(BF)
            for c in (0, 1):
                for h in (0, 1):
                    at = 192 * c + 96 * h
                    d_part[h, c, k] = product[at : at + 96]
            return carry

        lax.fori_loop(0, 4, body, 0)

    def split(product, target):
        for g in range(N):
            target[g % 2, g // 2] = product[48 * g : 48 * g + 48]

    def grad_qkv():
        gq.complete()
        split(dot(normed_t[...], qkv[:, 0:QA]).astype(BF), qa_part)
        split(dot(normed_t[...], qkv[:, QA:QW]).astype(BF), qb_part)

    def grad_up(b):
        def run():
            gp[b].complete()
            product = dot(normed_t[...], gpre[b]).astype(BF)
            split(product[:, 0:WIDE], uw_part.at[b])
            split(product[:, WIDE:DM], un_part.at[b])

        return run

    def input_qkv():
        gq.complete()
        wq.complete()

        def body(i, carry):
            r = pl.ds(pl.multiple_of(i * 256, 256), 256)
            summed[r] = dot_bt(qkv[r], w_qkv[...])
            return carry

        lax.fori_loop(0, 2, body, 0)

    plane = {}

    def input_up():
        wu.complete()

        def body(i, carry):
            r = pl.ds(pl.multiple_of(i * 256, 256), 256)
            total = summed[r]
            for b in range(4):
                total = total + dot_bt(gpre[b, r], w_up[:, b * DM : b * DM + DM])
            outgoing[r] = total.astype(BF)
            return carry

        for b in range(4):
            gp[b].complete()
        lax.fori_loop(0, 2, body, 0)
        plane["x"] = [
            Send(outgoing.at[rows_of(z * 4 + x_index(d), ROWS)], in_x.at[d - 1, z], xs[d - 1])
            for d in (1, 2, 3)
            for z in (0, 1)
        ]

    def plane_total(z):
        total = outgoing[rows_of(z * 4 + x, ROWS)].astype(F32)
        for d in range(3):
            total = total + in_x[d, z].astype(F32)
        return total

    def plane_forward():
        wait_all(plane["x"])
        rows = rows_of((1 - z_lo) * 4 + x, ROWS)
        outgoing[rows] = plane_total(1 - z_lo).astype(BF)
        plane["z"] = Send(outgoing.at[rows], in_z, zp)

    def plane_finish():
        plane["z"].wait()
        gi_out[...] = (plane_total(z_lo) + in_z[...].astype(F32)).astype(BF)
        load(gi_out, gi_hbm)

    def store_down(h, value):
        gwd_out[96 * h : 96 * h + 96] = value
        if h == 1:
            load(gwd_out, gwd_hbm)

    def store_qkv(h, value):
        cols = slice(0, QA) if h == 0 else slice(QA, QW)
        gwq_out[:, cols] = value
        if h == 1:
            load(gwq_out, gwq_hbm)

    def store_up(b):
        def store(h, value):
            at = b * DM + (WIDE if narrow(b) == h else 0)
            gwu_out[:, at : at + value.shape[1]] = value
            if h == 1:
                cols = pl.ds(b * DM, DM)
                load(gwu_out.at[:, cols], gwu_hbm.at[:, cols])

        return store

    def narrow(b):
        return 1 - b % 2

    def up_halves(b):
        halves = [(uw_part.at[b], uw_sib.at[b], uw_first.at[b], uw_last.at[b]),
                  (un_part.at[b], un_sib.at[b], un_first.at[b], un_last.at[b])]
        return halves if b % 2 == 0 else halves[::-1]

    wd = ChipGather(wd_in, w_down, 192, True)
    wu, wq = ChipGather(wu_in, w_up, 48, False), ChipGather(wq_in, w_qkv, 48, False)
    ga, gq, gp = RingGather(act), RingGather(qkv, q_in), [BlockGather(gpre.at[b]) for b in range(4)]
    rr = [RingReduce(rel) for rel in range(4)]
    pg, pn = PlaneGather(g_in, grads), PlaneGather(n_in, normed)
    rd = ChipReduce([(d_part.at[h], d_sib.at[h], d_first.at[h], d_last.at[h]) for h in (0, 1)], grad_down, store_down)
    ru = [ChipReduce(up_halves(b), grad_up(b), store_up(b)) for b in range(4)]
    rq = ChipReduce([(qa_part, qa_sib, qa_first, qa_last), (qb_part, qb_sib, qb_first, qb_last)], grad_qkv, store_qkv)

    load_pre = load(p_in, pre)
    load(q_in, qkv.at[rows_of(gy, ROWS)])
    load(g_in, grads.at[rows_of(gz, ROWS)])
    load(wd_in, w_down.at[rows_of(gx, 192)])
    load(n_in, normed.at[rows_of(gz, ROWS)])
    load(wu_in, w_up.at[rows_of(gx, 48)])
    load(wq_in, w_qkv.at[rows_of(gx, 48)])
    load_pre.wait()
    gelu()
    for copy in loads[1:]:
        copy.wait()
    first_store = len(loads)
    pl.semaphore_wait(barrier, len(peers))

    ga.go(0,0)
    ga.go(1,1)
    ga.go(0,1)
    ga.go(1,0)
    wd.start()
    pg.start()
    pn.start()
    gq.go(0,0)
    gq.go(1,1)
    ga.go(0,0)
    ga.go(1,1)
    ga.go(0,1)
    ga.go(1,0)
    wd.fwd_r()
    wd.fwd_l()
    gq.go(0,1)
    gq.go(1,0)
    wd.sh_r()
    wd.sh_l()
    ga.go(0,0)
    ga.go(1,1)
    pg.forward()
    pn.forward()
    ga.go(0,1)
    ga.go(1,0)
    wu.start()
    wd.far_l()
    gq.go(0,0)
    gq.go(1,1)
    rr[0].start()
    ga.go(0,0)
    ga.go(1,1)
    wd.far_r()
    rr[1].start()
    rr[2].start()
    rr[3].start()
    rr[0].up()
    rr[0].down()
    tn()
    gq.go(0,1)
    gq.go(1,0)
    rd.start()
    rr[0].up()
    rr[0].down()
    rr[1].up()
    rr[1].down()
    rr[2].up()
    rr[2].down()
    rr[3].up()
    rr[3].down()
    wu.fwd_r()
    wu.fwd_l()
    rr[0].up()
    rd.chips()
    rr[0].down()
    rr[1].up()
    rr[1].down()
    rr[2].up()
    rr[2].down()
    rr[3].up()
    rr[3].down()
    gq.go(0,0)
    rr[0].finish()
    wu.far_r()
    wu.far_l()
    gq.go(1,1)
    rr[1].up()
    rr[1].down()
    rr[2].up()
    rr[2].down()
    rr[3].up()
    rr[3].down()
    rd.fwd_r()
    rd.fwd_l()
    gq.go(0,1)
    gq.go(1,0)
    rr[1].finish()
    gq.go(0,0)
    gq.go(1,1)
    rr[2].finish()
    rr[3].finish()
    gp[0].start()
    gp[1].start()
    gp[2].start()
    gp[3].start()
    wq.start()
    rd.finish()
    rq.start()
    gp[0].up()
    gp[0].down()
    gp[1].up()
    gp[1].down()
    gp[2].up()
    gp[2].down()
    gp[3].up()
    gp[3].down()
    rq.chips()
    gp[0].up()
    gp[0].down()
    wq.fwd_r()
    wq.fwd_l()
    gp[1].up()
    gp[1].down()
    gp[2].up()
    gp[2].down()
    gp[3].up()
    gp[3].down()
    gp[0].up()
    gp[0].down()
    rq.fwd_r()
    rq.fwd_l()
    gp[1].up()
    gp[1].down()
    gp[2].up()
    gp[2].down()
    gp[3].up()
    gp[3].down()
    ru[0].start()
    ru[1].start()
    ru[2].start()
    wq.far_r()
    wq.far_l()
    ru[3].start()
    ru[0].chips()
    ru[1].chips()
    ru[2].chips()
    rq.finish()
    input_qkv()
    input_up()
    ru[0].fwd_r()
    ru[0].fwd_l()
    ru[1].fwd_r()
    ru[1].fwd_l()
    ru[3].chips()
    ru[2].fwd_r()
    ru[2].fwd_l()
    ru[0].finish()
    ru[1].finish()
    ru[3].fwd_r()
    ru[3].fwd_l()
    plane_forward()
    ru[2].finish()
    ru[3].finish()
    plane_finish()
    for copy in loads[first_store:]:
        copy.wait()
    for sent in started:
        sent.copy.wait_send()


def reduce_scratch(rows, width, *lead):
    return [
        pltpu.VMEM(lead + (2, 4, rows, width), BF),
        pltpu.VMEM(lead + (4, rows, width), BF),
        pltpu.VMEM(lead + (rows, width), BF),
        pltpu.VMEM(lead + (2, rows, width), BF),
    ]


def shards(normed, grad_out, grad_qkv_out, pre_act, w_qkv, w_up, w_down):
    outs = (normed, w_qkv, w_up, w_down)
    return pl.pallas_call(
        kernel,
        out_shape=[jax.ShapeDtypeStruct(o.shape, BF) for o in outs],
        in_specs=[pl.BlockSpec(memory_space=pltpu.HBM)] * 7,
        out_specs=[pl.BlockSpec(memory_space=pltpu.HBM)] * 4,
        scratch_shapes=[
            pltpu.VMEM((N * ROWS, DM), BF),
            pltpu.VMEM((DM, N * ROWS), BF),
            pltpu.VMEM((N * ROWS, DM), BF),
            pltpu.VMEM((N * ROWS, QW), BF),
            pltpu.VMEM((N * ROWS, FW), BF),
            pltpu.VMEM((4, ROWS, DM), F32),
            pltpu.VMEM((FW, DM), BF),
            pltpu.VMEM((DM, FW), BF),
            pltpu.VMEM((DM, QW), BF),
            pltpu.VMEM((4, N * ROWS, DM), BF),
            pltpu.VMEM((4, 4, ROWS, DM), BF),
            pltpu.VMEM((4, 4, ROWS, DM), BF),
            pltpu.VMEM((4, N * ROWS, DM), BF),
            pltpu.VMEM((N * ROWS, DM), F32),
            pltpu.VMEM((N * ROWS, DM), BF),
            pltpu.VMEM((3, 2, ROWS, DM), BF),
            pltpu.VMEM((ROWS, DM), BF),
            *reduce_scratch(96, DM, 2),
            *reduce_scratch(48, WIDE, 4),
            *reduce_scratch(48, DM - WIDE, 4),
            *reduce_scratch(48, QA),
            *reduce_scratch(48, QB),
            pltpu.VMEM((ROWS, FW), BF),
            *[pltpu.VMEM(o.shape, BF) for o in outs],
            pltpu.SemaphoreType.DMA((COPIES,)),
            pltpu.SemaphoreType.DMA((COPIES,)),
            pltpu.SemaphoreType.DMA((16,)),
        ],
        compiler_params=pltpu.CompilerParams(
            collective_id=0, has_side_effects=True, vmem_limit_bytes=60 << 20
        ),
    )(normed, grad_out, grad_qkv_out, pre_act, w_qkv, w_up, w_down)


def solution(mesh):
    rows, tall = P(("gx", "gz"), "gy"), P(("gx", "gy"), "gz")
    block, flat = P(("gy", "gx"), "gz"), P(("gz", "gx"), "gy")
    return jax.shard_map(
        shards,
        mesh=mesh,
        in_specs=(rows, rows, tall, tall, block, block, flat),
        out_specs=(rows, block, block, flat),
        check_vma=False,
    )
```

```python
import math

import jax
import jax.numpy as jnp
from jax import lax
from jax.experimental import pallas as pl
from jax.experimental.pallas import tpu as pltpu
from jax.sharding import PartitionSpec as P

MESH = pl.DeviceIdType.MESH
BF = jnp.bfloat16
F32 = jnp.float32
N = 8
ROWS = 64
HALF = 32
DM = 384
QW = 1152
FW = 1536
QA = 640
QB = 512
WIDE = 256
COPIES = 143
RING, CHIP, CORE, PLANE = range(4)
LINKS = 4


def dot_bt(a, b):
    return lax.dot_general(a, b, (((1,), (1,)), ((), ())), preferred_element_type=F32)


def dot_ta(a, b):
    return lax.dot_general(a, b, (((0,), (0,)), ((), ())), preferred_element_type=F32)


def dot(a, b):
    return jnp.dot(a, b, preferred_element_type=F32)


def wrap(i):
    return lax.rem(i + 2 * N, N)


def rows_of(slot, size, start=0, count=None):
    count = size if count is None else count
    return pl.ds(pl.multiple_of(slot * size + start, 16), count)


def kernel(
    n_in, g_in, q_in, p_in, wq_in, wu_in, wd_in,
    gi_out, gwq_out, gwu_out, gwd_out,
    normed, normed_t, grads, qkv, act, slope, w_down, w_up, w_qkv,
    part, part_u, part_d, gpre, summed, outgoing, in_x, in_z,
    d_part, d_sib, d_first, d_last,
    uw_part, uw_sib, uw_first, uw_last,
    un_part, un_sib, un_first, un_last,
    qa_part, qa_sib, qa_first, qa_last,
    qb_part, qb_sib, qb_first, qb_last,
    pre, size_ref, send_sems, recv_sems, load_sems,
):
    gx, gy, gz = lax.axis_index("gx"), lax.axis_index("gy"), lax.axis_index("gz")
    core = lax.rem(gx, 2)
    chip = gx // 2
    z_lo, x = gz // 4, lax.rem(gz, 4)

    sib = (gx + 1 - 2 * core, gy, gz)
    chip_r, chip_l = (wrap(gx + 2), gy, gz), (wrap(gx - 2), gy, gz)
    up, down = (gx, wrap(gy + 1), gz), (gx, wrap(gy - 1), gz)
    zp = (gx, gy, wrap(gz + 4))

    def x_index(shift):
        return lax.rem(x + shift, 4)

    xs = [(gx, gy, z_lo * 4 + x_index(d)) for d in (1, 2, 3)]

    barrier = pltpu.get_barrier_semaphore()
    peers = [sib, chip_r, chip_l, up, down, zp] + xs
    for peer in peers:
        pl.semaphore_signal(barrier, inc=1, device_id=peer, device_id_type=MESH)

    loads = []

    def load(src, dst):
        copy = pltpu.make_async_copy(src, dst, load_sems.at[len(loads)])
        copy.start()
        loads.append(copy)
        return copy

    sent = [0] * LINKS
    landings = []

    def wait_bytes(count, sem):
        piece = size_ref.at[pl.ds(0, count // 256)]
        pltpu.make_async_copy(piece, piece, sem).wait()

    class Landing:
        def __init__(self):
            self.sem = recv_sems.at[len(landings)]
            self.bytes = 0
            self.done = False
            landings.append(self)

        def wait(self):
            if not self.done:
                wait_bytes(self.bytes, self.sem)
            self.done = True

    def send(src, dst, peer, link, landing=None):
        landing = Landing() if landing is None else landing
        assert not landing.done
        pltpu.make_async_remote_copy(
            src_ref=src, dst_ref=dst, send_sem=send_sems.at[link], recv_sem=landing.sem,
            device_id=peer, device_id_type=MESH,
        ).start()
        size = 2 * math.prod(src.shape)
        landing.bytes += size
        sent[link] += size
        return landing

    def wait_all(copies):
        for copy in copies:
            copy.wait()

    class ChipGather:
        def __init__(self, own, full, size):
            self.own, self.full, self.size = own, full, size
            self.to_sib = Landing()
            self.count = 0

        def half_at(self, h):
            if self.size % 32 == 0:
                return (pl.ds(h * self.size // 2, self.size // 2),)
            width = self.full.shape[1] // 256 * 128
            return (slice(None), pl.ds(0, width) if h == 0 else pl.ds(width, self.full.shape[1] - width))

        def at(self, shift):
            return self.full.at[rows_of(wrap(gx + shift), self.size)]

        def half(self, shift, h):
            return self.at(shift).at[self.half_at(h)]

        def share(self, src, dst):
            self.count += 1
            send(src, dst, sib, CORE, self.to_sib)

        def start_a(self):
            self.r = [send(self.own.at[self.half_at(0)], self.half(0, 0), chip_r, CHIP)]
            self.l = [send(self.own.at[self.half_at(1)], self.half(0, 1), chip_l, CHIP)]
            self.share(self.own, self.at(0))

        def start_b(self):
            self.r.append(send(self.own.at[self.half_at(1)], self.half(0, 1), chip_r, CHIP))
            self.l.append(send(self.own.at[self.half_at(0)], self.half(0, 0), chip_l, CHIP))

        def fwd_r(self):
            self.r[0].wait()
            self.far_up = send(self.half(-2, 0), self.half(-2, 0), chip_r, CHIP)

        def fwd_l(self):
            self.l[0].wait()
            self.far_down = send(self.half(2, 1), self.half(2, 1), chip_l, CHIP)

        def sh_r(self):
            wait_all(self.r)
            self.share(self.at(-2), self.at(-2))

        def sh_l(self):
            wait_all(self.l)
            self.share(self.at(2), self.at(2))

        def far_r(self):
            self.far_up.wait()
            self.share(self.half(4, 0), self.half(4, 0))

        def far_l(self):
            self.far_down.wait()
            self.share(self.half(4, 1), self.half(4, 1))

        def complete(self):
            assert self.count == 5
            self.to_sib.wait()

    class RingGather:
        def __init__(self, full, own=None):
            self.full, self.own = full, own
            self.chain = {}
            self.hops = {}

        def at(self, shift, h):
            return self.full.at[rows_of(wrap(gy + shift), ROWS, HALF * h, HALF)]

        def go(self, d, h):
            s = self.hops.get((d, h), 0)
            self.hops[d, h] = s + 1
            if s > 0:
                self.chain[d, h].wait()
            here = self.at(s if d else -s, h)
            src = self.own.at[pl.ds(HALF * h, HALF)] if s == 0 and self.own is not None else here
            self.chain[d, h] = send(src, here, down if d else up, RING)

        def complete(self):
            assert self.hops == {(0, 0): 4, (1, 1): 4, (0, 1): 3, (1, 0): 3}
            for key in self.chain:
                self.chain[key].wait()

    class BlockGather:
        def __init__(self, full):
            self.full = full

        def at(self, shift, start=0, count=ROWS):
            return self.full.at[rows_of(wrap(gy + shift), ROWS, start, count)]

        def start(self):
            self.step_u = self.step_d = 0
            self.to_u = send(self.at(0), self.at(0), up, RING)
            self.to_d = send(self.at(0), self.at(0), down, RING)

        def up(self):
            self.step_u += 1
            self.to_u.wait()
            src = self.at(-self.step_u, 0, ROWS if self.step_u < 3 else HALF)
            self.to_u = send(src, src, up, RING)

        def down(self):
            self.step_d += 1
            self.to_d.wait()
            src = self.at(self.step_d) if self.step_d < 3 else self.at(3, HALF, HALF)
            self.to_d = send(src, src, down, RING)

        def complete(self):
            assert self.step_u == self.step_d == 3
            self.to_u.wait()
            self.to_d.wait()

    class RingReduce:
        def __init__(self, block):
            self.block = block
            self.mine = part.at[self.block]

        def at(self, shift, start=0, count=ROWS):
            return rows_of(wrap(gy + shift), ROWS, start, count)

        def start(self):
            pg.complete()
            wd.complete()
            rows = rows_of(self.block, DM)

            def body(i, carry):
                r = pl.ds(pl.multiple_of(i * 256, 256), 256)
                self.mine[r] = dot_bt(grads[r], w_down[rows]).astype(BF)
                return carry

            lax.fori_loop(0, 2, body, 0)
            self.step_u = self.step_d = 1
            first = pl.ds(0, HALF), pl.ds(HALF, HALF)
            self.to_u = send(self.mine.at[self.at(4, 0, HALF)], part_u.at[self.block, 0, first[0]], up, RING)
            self.to_d = send(self.mine.at[self.at(4, HALF, HALF)], part_d.at[self.block, 0, first[1]], down, RING)

        def add(self, rows, other):
            self.mine[rows] = (self.mine[rows].astype(F32) + other.astype(F32)).astype(BF)

        def up(self):
            s = self.step_u
            self.step_u += 1
            self.to_u.wait()
            if s == 1:
                self.add(self.at(3, 0, HALF), part_u[self.block, 0, 0:HALF])
            else:
                self.add(self.at(4 - s), part_u[self.block, s - 1])
            self.to_u = send(self.mine.at[self.at(4 - s)], part_u.at[self.block, s], up, RING)

        def down(self):
            s = self.step_d
            self.step_d += 1
            self.to_d.wait()
            if s == 1:
                self.add(self.at(-3, HALF, HALF), part_d[self.block, 0, HALF:ROWS])
            else:
                self.add(self.at(s - 4), part_d[self.block, s - 1])
            self.to_d = send(self.mine.at[self.at(s - 4)], part_d.at[self.block, s], down, RING)

        def finish(self):
            assert self.step_u == self.step_d == 4
            self.to_u.wait()
            self.to_d.wait()
            rows = self.at(0)
            total = self.mine[rows].astype(F32) + part_u[self.block, 3].astype(F32) + part_d[self.block, 3].astype(F32)
            gpre[self.block, rows] = (total * slope[self.block]).astype(BF)

    class PlaneGather:
        def __init__(self, own, full):
            self.own, self.full = own, full

        def at(self, shift):
            return self.full.at[rows_of(wrap(gz + shift), ROWS)]

        def start(self):
            self.to_z = send(self.own, self.at(0), zp, PLANE)
            self.to_x = Landing()
            self.spread(self.own, 0)

        def forward(self):
            self.to_z.wait()
            self.spread(self.at(4), 4)
            self.ready = True

        def spread(self, src, shift):
            for peer in xs:
                send(src, self.at(shift), peer, PLANE, self.to_x)

        def complete(self):
            assert self.ready
            self.to_x.wait()

    class ChipReduce:
        def __init__(self, halves, compute, store):
            self.halves, self.compute, self.store = halves, compute, store

        def start(self):
            self.compute()
            self.swap = Landing()
            for p, s, _, _ in self.halves:
                send(p.at[1 - core], s, sib, CORE, self.swap)

        def total(self, h, k):
            p, s, _, _ = self.halves[h]
            return p[core, k].astype(F32) + s[k].astype(F32)

        def put(self, h, k, value):
            self.halves[h][0][core, k] = value.astype(BF)

        def chips(self):
            self.swap.wait()
            far, right, left = (lax.rem(chip + i, 4) for i in (2, 1, 3))
            (pa, _, fa, la), (pb, _, fb, lb) = self.halves
            self.put(0, far, self.total(0, far))
            self.far_up = send(pa.at[core, far], fa, chip_r, CHIP)
            self.put(1, far, self.total(1, far))
            self.far_down = send(pb.at[core, far], fb, chip_l, CHIP)
            self.put(1, right, self.total(1, right))
            self.near = send(pb.at[core, right], lb.at[0], chip_r, CHIP)
            self.put(0, left, self.total(0, left))
            send(pa.at[core, left], la.at[1], chip_l, CHIP, self.near)

        def fwd_r(self):
            right = lax.rem(chip + 1, 4)
            pa, _, fa, la = self.halves[0]
            self.far_up.wait()
            self.put(0, right, self.total(0, right) + fa[...].astype(F32))
            send(pa.at[core, right], la.at[0], chip_r, CHIP, self.near)

        def fwd_l(self):
            left = lax.rem(chip + 3, 4)
            pb, _, fb, lb = self.halves[1]
            self.far_down.wait()
            self.put(1, left, self.total(1, left) + fb[...].astype(F32))
            send(pb.at[core, left], lb.at[1], chip_l, CHIP, self.near)

        def finish(self):
            self.near.wait()
            for h in (0, 1):
                last = self.halves[h][3]
                self.store(h, (self.total(h, chip) + last[0].astype(F32) + last[1].astype(F32)).astype(BF))

    def gelu():
        def body(i, carry):
            r = pl.ds(pl.multiple_of(i * 16, 16), 16)
            for b in range(4):
                cols = slice(b * DM, b * DM + DM)
                v = pre[r, cols].astype(F32)
                cdf = 0.5 * (1.0 + lax.erf(v * 0.7071067811865476))
                pdf = jnp.exp(-0.5 * v * v) * 0.3989422804014327
                act[rows_of(gy, ROWS, i * 16, 16), cols] = (v * cdf).astype(BF)
                slope[b, r] = cdf + v * pdf
            return carry

        lax.fori_loop(0, ROWS // 16, body, 0)

    def tn():
        pn.complete()
        normed_t[...] = normed[...].T

    def grad_down():
        ga.complete()
        pg.complete()

        def body(k, carry):
            cols = pl.ds(pl.multiple_of(k * DM, DM), DM)
            product = dot_ta(act[:, cols], grads[...]).astype(BF)
            for c in (0, 1):
                for h in (0, 1):
                    at = 192 * c + 96 * h
                    d_part[h, c, k] = product[at : at + 96]
            return carry

        lax.fori_loop(0, 4, body, 0)

    def split(product, target):
        for g in range(N):
            target[g % 2, g // 2] = product[48 * g : 48 * g + 48]

    def grad_qkv():
        gq.complete()
        split(dot(normed_t[...], qkv[:, 0:QA]).astype(BF), qa_part)
        split(dot(normed_t[...], qkv[:, QA:QW]).astype(BF), qb_part)

    def grad_up(b):
        def run():
            gp[b].complete()
            product = dot(normed_t[...], gpre[b]).astype(BF)
            split(product[:, 0:WIDE], uw_part.at[b])
            split(product[:, WIDE:DM], un_part.at[b])

        return run

    def input_qkv():
        gq.complete()
        wq.complete()

        def body(i, carry):
            r = pl.ds(pl.multiple_of(i * 256, 256), 256)
            summed[r] = dot_bt(qkv[r], w_qkv[...])
            return carry

        lax.fori_loop(0, 2, body, 0)

    plane = {}

    def input_up(b):
        gp[b].complete()
        wu.complete()

        def body(i, carry):
            r = pl.ds(pl.multiple_of(i * 256, 256), 256)
            total = summed[r] + dot_bt(gpre[b, r], w_up[:, b * DM : b * DM + DM])
            if b < 3:
                summed[r] = total
            else:
                outgoing[r] = total.astype(BF)
            return carry

        lax.fori_loop(0, 2, body, 0)

    def plane_start():
        plane["x"] = Landing()
        for d in (1, 2, 3):
            for z in (0, 1):
                rows = rows_of(z * 4 + x_index(d), ROWS)
                send(outgoing.at[rows], in_x.at[d - 1, z], xs[d - 1], PLANE, plane["x"])

    def plane_total(z):
        total = outgoing[rows_of(z * 4 + x, ROWS)].astype(F32)
        for d in range(3):
            total = total + in_x[d, z].astype(F32)
        return total

    def plane_forward():
        plane["x"].wait()
        rows = rows_of((1 - z_lo) * 4 + x, ROWS)
        outgoing[rows] = plane_total(1 - z_lo).astype(BF)
        plane["z"] = send(outgoing.at[rows], in_z, zp, PLANE)

    def plane_finish():
        plane["z"].wait()
        gi_out[...] = (plane_total(z_lo) + in_z[...].astype(F32)).astype(BF)

    def store_down(h, value):
        gwd_out[96 * h : 96 * h + 96] = value

    def store_qkv(h, value):
        cols = slice(0, QA) if h == 0 else slice(QA, QW)
        gwq_out[:, cols] = value

    def store_up(b):
        def store(h, value):
            at = b * DM + (WIDE if narrow(b) == h else 0)
            gwu_out[:, at : at + value.shape[1]] = value

        return store

    def narrow(b):
        return 1 - b % 2

    def up_halves(b):
        halves = [(uw_part.at[b], uw_sib.at[b], uw_first.at[b], uw_last.at[b]),
                  (un_part.at[b], un_sib.at[b], un_first.at[b], un_last.at[b])]
        return halves if b % 2 == 0 else halves[::-1]

    wd = ChipGather(wd_in, w_down, 192)
    wu, wq = ChipGather(wu_in, w_up, 48), ChipGather(wq_in, w_qkv, 48)
    ga, gq, gp = RingGather(act), RingGather(qkv, q_in), [BlockGather(gpre.at[b]) for b in range(4)]
    rr = [RingReduce(b) for b in range(4)]
    pg, pn = PlaneGather(g_in, grads), PlaneGather(n_in, normed)
    rd = ChipReduce([(d_part.at[h], d_sib.at[h], d_first.at[h], d_last.at[h]) for h in (0, 1)], grad_down, store_down)
    ru = [ChipReduce(up_halves(b), grad_up(b), store_up(b)) for b in range(4)]
    rq = ChipReduce([(qa_part, qa_sib, qa_first, qa_last), (qb_part, qb_sib, qb_first, qb_last)], grad_qkv, store_qkv)

    load_pre = load(p_in, pre)
    load(q_in, qkv.at[rows_of(gy, ROWS)])
    load(g_in, grads.at[rows_of(gz, ROWS)])
    load(wd_in, w_down.at[rows_of(gx, 192)])
    load(n_in, normed.at[rows_of(gz, ROWS)])
    load(wu_in, w_up.at[rows_of(gx, 48)])
    load(wq_in, w_qkv.at[rows_of(gx, 48)])
    load_pre.wait()
    gelu()
    for copy in loads[1:]:
        copy.wait()
    pl.semaphore_wait(barrier, len(peers))

    gq.go(0,0)
    gq.go(1,0)
    pn.start()
    gq.go(1,1)
    gq.go(0,1)
    pg.start()
    wd.start_a()
    ga.go(0,0)
    ga.go(1,0)
    wd.start_b()
    gq.go(0,0)
    gq.go(1,0)
    pn.forward()
    pg.forward()
    gq.go(1,1)
    gq.go(0,1)
    ga.go(0,1)
    ga.go(1,1)
    wd.fwd_l()
    wd.fwd_r()
    tn()
    gq.go(0,0)
    gq.go(1,0)
    gq.go(0,1)
    gq.go(1,1)
    wd.sh_l()
    wd.sh_r()
    ga.go(0,0)
    ga.go(1,0)
    wu.start_a()
    gq.go(0,0)
    ga.go(1,1)
    wd.far_l()
    wd.far_r()
    ga.go(0,1)
    wu.start_b()
    gq.go(1,1)
    rr[0].start()
    rr[1].start()
    rr[2].start()
    wq.start_a()
    ga.go(0,0)
    ga.go(1,0)
    wu.fwd_r()
    wu.fwd_l()
    rr[3].start()
    rq.start()
    rr[0].up()
    rr[0].down()
    rr[1].up()
    rr[1].down()
    wu.sh_r()
    rr[2].up()
    rr[2].down()
    wu.sh_l()
    rq.chips()
    wq.fwd_r()
    wq.fwd_l()
    ga.go(0,1)
    ga.go(1,1)
    rr[3].up()
    rr[3].down()
    rr[0].up()
    rr[0].down()
    rr[1].up()
    rr[1].down()
    wu.far_r()
    wu.far_l()
    rr[2].up()
    rr[2].down()
    rq.fwd_r()
    rq.fwd_l()
    ga.go(0,0)
    ga.go(1,1)
    rr[3].up()
    rr[3].down()
    rr[0].up()
    rr[0].down()
    rr[1].up()
    rr[1].down()
    rr[2].up()
    rr[2].down()
    wq.start_b()
    wq.far_r()
    wq.far_l()
    rd.start()
    rq.finish()
    rr[0].finish()
    gp[0].start()
    rr[3].up()
    rr[3].down()
    rr[1].finish()
    gp[1].start()
    rd.chips()
    rr[2].finish()
    gp[2].start()
    wq.sh_r()
    wq.sh_l()
    gp[0].up()
    gp[0].down()
    rr[3].finish()
    gp[3].start()
    input_qkv()
    gp[1].up()
    gp[1].down()
    gp[2].up()
    gp[2].down()
    gp[0].up()
    gp[0].down()
    gp[3].up()
    gp[3].down()
    rd.fwd_r()
    rd.fwd_l()
    gp[1].up()
    gp[1].down()
    gp[2].up()
    gp[2].down()
    gp[0].up()
    gp[0].down()
    gp[3].up()
    gp[3].down()
    gp[1].up()
    gp[1].down()
    gp[2].up()
    gp[2].down()
    ru[0].start()
    rd.finish()
    input_up(0)
    gp[3].up()
    gp[3].down()
    ru[1].start()
    ru[0].chips()
    ru[2].start()
    input_up(1)
    ru[1].chips()
    ru[3].start()
    ru[2].chips()
    input_up(2)
    input_up(3)
    plane_start()
    ru[3].chips()
    ru[0].fwd_r()
    ru[0].fwd_l()
    ru[1].fwd_r()
    ru[1].fwd_l()
    ru[2].fwd_r()
    ru[2].fwd_l()
    ru[3].fwd_r()
    ru[3].fwd_l()
    plane_forward()
    ru[0].finish()
    ru[1].finish()
    ru[2].finish()
    ru[3].finish()
    plane_finish()
    assert len(landings) <= COPIES
    for link in range(LINKS):
        wait_bytes(sent[link], send_sems.at[link])


def reduce_scratch(rows, width, *lead):
    return [
        pltpu.VMEM(lead + (2, 4, rows, width), BF),
        pltpu.VMEM(lead + (4, rows, width), BF),
        pltpu.VMEM(lead + (rows, width), BF),
        pltpu.VMEM(lead + (2, rows, width), BF),
    ]


def shards(normed, grad_out, grad_qkv_out, pre_act, w_qkv, w_up, w_down):
    ins, outs = (normed, grad_out, grad_qkv_out, pre_act, w_qkv, w_up, w_down), (normed, w_qkv, w_up, w_down)
    return pl.pallas_call(
        kernel,
        out_shape=[pltpu.VMEM(o.shape, BF) for o in outs],
        in_specs=[pl.BlockSpec(memory_space=pltpu.HBM)] * 7,
        out_specs=[pl.BlockSpec(memory_space=pltpu.VMEM)] * 4,
        scratch_shapes=[
            pltpu.VMEM((N * ROWS, DM), BF),
            pltpu.VMEM((DM, N * ROWS), BF),
            pltpu.VMEM((N * ROWS, DM), BF),
            pltpu.VMEM((N * ROWS, QW), BF),
            pltpu.VMEM((N * ROWS, FW), BF),
            pltpu.VMEM((4, ROWS, DM), F32),
            pltpu.VMEM((FW, DM), BF),
            pltpu.VMEM((DM, FW), BF),
            pltpu.VMEM((DM, QW), BF),
            pltpu.VMEM((4, N * ROWS, DM), BF),
            pltpu.VMEM((4, 4, ROWS, DM), BF),
            pltpu.VMEM((4, 4, ROWS, DM), BF),
            pltpu.VMEM((4, N * ROWS, DM), BF),
            pltpu.VMEM((N * ROWS, DM), F32),
            pltpu.VMEM((N * ROWS, DM), BF),
            pltpu.VMEM((3, 2, ROWS, DM), BF),
            pltpu.VMEM((ROWS, DM), BF),
            *reduce_scratch(96, DM, 2),
            *reduce_scratch(48, WIDE, 4),
            *reduce_scratch(48, DM - WIDE, 4),
            *reduce_scratch(48, QA),
            *reduce_scratch(48, QB),
            pltpu.VMEM((ROWS, FW), BF),
            pltpu.VMEM((24 << 10, 128), BF),
            pltpu.SemaphoreType.DMA((LINKS,)),
            pltpu.SemaphoreType.DMA((COPIES,)),
            pltpu.SemaphoreType.DMA((7,)),
        ],
        compiler_params=pltpu.CompilerParams(
            collective_id=0, has_side_effects=True, vmem_limit_bytes=48 << 20
        ),
    )(*[pltpu.with_memory_space_constraint(a, pltpu.HBM) for a in ins])


def solution(mesh):
    rows, tall = P(("gx", "gz"), "gy"), P(("gx", "gy"), "gz")
    block, flat = P(("gy", "gx"), "gz"), P(("gz", "gx"), "gy")
    return jax.shard_map(
        shards,
        mesh=mesh,
        in_specs=(rows, rows, tall, tall, block, block, flat),
        out_specs=(rows, block, block, flat),
        check_vma=False,
    )
```

```python
import math

import jax
import jax.numpy as jnp
from jax import lax
from jax.experimental import pallas as pl
from jax.experimental.pallas import tpu as pltpu
from jax.sharding import PartitionSpec as P

MESH = pl.DeviceIdType.MESH
BF = jnp.bfloat16
F32 = jnp.float32
N = 8
ROWS = 64
HALF = 32
DM = 384
QW = 1152
FW = 1536
QA = 640
QB = 512
WIDE = 256
COPIES = 84
RING, CHIP, CORE, PLANE = range(4)
LINKS = 4


def dot_bt(a, b):
    return lax.dot_general(a, b, (((1,), (1,)), ((), ())), preferred_element_type=F32)


def dot_ta(a, b):
    return lax.dot_general(a, b, (((0,), (0,)), ((), ())), preferred_element_type=F32)


def dot(a, b):
    return jnp.dot(a, b, preferred_element_type=F32)


def wrap(i):
    return lax.rem(i + 2 * N, N)


def rows_of(slot, size, start=0, count=None):
    count = size if count is None else count
    return pl.ds(pl.multiple_of(slot * size + start, 16), count)


def kernel(
    n_in, g_in, q_in, p_in, wq_in, wu_in, wd_in,
    gi_out, gwq_out, gwu_out, gwd_out,
    normed, normed_t, grads, qkv, act, slope, w_down, w_up, w_qkv,
    part, part_u, part_d, gpre, summed, outgoing, in_x, in_z,
    d_part, d_sib, d_first, d_last,
    uw_part, uw_sib, uw_first, uw_last,
    un_part, un_sib, un_first, un_last,
    qa_part, qa_sib, qa_first, qa_last,
    qb_part, qb_sib, qb_first, qb_last,
    pre, size_ref, send_sems, recv_sems, load_sems,
):
    gx, gy, gz = lax.axis_index("gx"), lax.axis_index("gy"), lax.axis_index("gz")
    core = lax.rem(gx, 2)
    chip = gx // 2
    z_lo, x = gz // 4, lax.rem(gz, 4)

    sib = (gx + 1 - 2 * core, gy, gz)
    chip_r, chip_l = (wrap(gx + 2), gy, gz), (wrap(gx - 2), gy, gz)
    up, down = (gx, wrap(gy + 1), gz), (gx, wrap(gy - 1), gz)
    zp = (gx, gy, wrap(gz + 4))

    def x_index(shift):
        return lax.rem(x + shift, 4)

    xs = [(gx, gy, z_lo * 4 + x_index(d)) for d in (1, 2, 3)]

    barrier = pltpu.get_barrier_semaphore()
    peers = [sib, chip_r, chip_l, up, down, zp] + xs
    for peer in peers:
        pl.semaphore_signal(barrier, inc=1, device_id=peer, device_id_type=MESH)

    loads = []

    def load(src, dst):
        copy = pltpu.make_async_copy(src, dst, load_sems.at[len(loads)])
        copy.start()
        loads.append(copy)
        return copy

    sent = [0] * LINKS
    landings = []

    def wait_bytes(count, sem):
        piece = size_ref.at[pl.ds(0, count // 256)]
        pltpu.make_async_copy(piece, piece, sem).wait()

    class Landing:
        def __init__(self):
            self.sem = recv_sems.at[len(landings)]
            self.bytes = 0
            self.done = False
            landings.append(self)

        def wait(self):
            if not self.done:
                wait_bytes(self.bytes, self.sem)
            self.done = True

    def send(src, dst, peer, link, landing=None):
        landing = Landing() if landing is None else landing
        assert not landing.done
        pltpu.make_async_remote_copy(
            src_ref=src, dst_ref=dst, send_sem=send_sems.at[link], recv_sem=landing.sem,
            device_id=peer, device_id_type=MESH,
        ).start()
        size = 2 * math.prod(src.shape)
        landing.bytes += size
        sent[link] += size
        return landing

    def wait_all(copies):
        for copy in copies:
            copy.wait()

    class ChipGather:
        def __init__(self, own, full, size):
            self.own, self.full, self.size = own, full, size
            self.to_sib = Landing()
            self.count = 0

        def half_at(self, h):
            if self.size % 32 == 0:
                return (pl.ds(h * self.size // 2, self.size // 2),)
            width = self.full.shape[1] // 256 * 128
            return (slice(None), pl.ds(0, width) if h == 0 else pl.ds(width, self.full.shape[1] - width))

        def at(self, shift):
            return self.full.at[rows_of(wrap(gx + shift), self.size)]

        def half(self, shift, h):
            return self.at(shift).at[self.half_at(h)]

        def share(self, src, dst):
            self.count += 1
            send(src, dst, sib, CORE, self.to_sib)

        def start_a(self):
            self.a = send(self.own.at[self.half_at(0)], self.half(0, 0), chip_r, CHIP)
            send(self.own.at[self.half_at(1)], self.half(0, 1), chip_l, CHIP, self.a)
            self.share(self.own, self.at(0))

        def start_b(self):
            self.b = send(self.own.at[self.half_at(1)], self.half(0, 1), chip_r, CHIP)
            send(self.own.at[self.half_at(0)], self.half(0, 0), chip_l, CHIP, self.b)

        def fwd(self):
            self.a.wait()
            self.c = send(self.half(-2, 0), self.half(-2, 0), chip_r, CHIP)
            send(self.half(2, 1), self.half(2, 1), chip_l, CHIP, self.c)

        def sh(self):
            self.b.wait()
            self.share(self.at(-2), self.at(-2))
            self.share(self.at(2), self.at(2))

        def far(self):
            self.c.wait()
            self.share(self.half(4, 0), self.half(4, 0))
            self.share(self.half(4, 1), self.half(4, 1))

        def complete(self):
            assert self.count == 5
            self.to_sib.wait()

    class RingGather:
        def __init__(self, full, own=None):
            self.full, self.own = full, own
            self.chain = {}
            self.hops = {}

        def at(self, shift, h):
            return self.full.at[rows_of(wrap(gy + shift), ROWS, HALF * h, HALF)]

        def go(self, h):
            s = self.hops.get(h, 0)
            self.hops[h] = s + 1
            if s > 0:
                self.chain[h].wait()
            self.chain[h] = Landing()
            for d, peer in ((0, up), (1, down)):
                if s < 3 or d == h:
                    here = self.at(s if d else -s, h)
                    src = self.own.at[pl.ds(HALF * h, HALF)] if s == 0 and self.own is not None else here
                    send(src, here, peer, RING, self.chain[h])

        def complete(self):
            assert self.hops == {0: 4, 1: 4}
            for h in (0, 1):
                self.chain[h].wait()

    class BlockGather:
        def __init__(self, full):
            self.full = full

        def at(self, shift, start=0, count=ROWS):
            return self.full.at[rows_of(wrap(gy + shift), ROWS, start, count)]

        def start(self):
            self.step = 0
            self.go()

        def go(self):
            s = self.step
            self.step += 1
            if s > 0:
                self.landing.wait()
            self.landing = Landing()
            src = self.at(-s, 0, ROWS if s < 3 else HALF)
            send(src, src, up, RING, self.landing)
            src = self.at(s) if s < 3 else self.at(3, HALF, HALF)
            send(src, src, down, RING, self.landing)

        def complete(self):
            assert self.step == 4
            self.landing.wait()

    class RingReduce:
        def __init__(self, block):
            self.block = block
            self.mine = part.at[self.block]

        def at(self, shift, start=0, count=ROWS):
            return rows_of(wrap(gy + shift), ROWS, start, count)

        def start(self):
            pg.complete()
            wd.complete()
            rows = rows_of(self.block, DM)

            def body(i, carry):
                r = pl.ds(pl.multiple_of(i * 256, 256), 256)
                self.mine[r] = dot_bt(grads[r], w_down[rows]).astype(BF)
                return carry

            lax.fori_loop(0, 2, body, 0)
            self.step = 1
            half = self.at(4, 0, HALF), self.at(4, HALF, HALF)
            self.landing = send(self.mine.at[half[0]], part_u.at[self.block, 0, pl.ds(0, HALF)], up, RING)
            send(self.mine.at[half[1]], part_d.at[self.block, 0, pl.ds(HALF, HALF)], down, RING, self.landing)

        def add(self, rows, other):
            self.mine[rows] = (self.mine[rows].astype(F32) + other.astype(F32)).astype(BF)

        def go(self):
            s = self.step
            self.step += 1
            self.landing.wait()
            if s == 1:
                self.add(self.at(3, 0, HALF), part_u[self.block, 0, 0:HALF])
                self.add(self.at(-3, HALF, HALF), part_d[self.block, 0, HALF:ROWS])
            else:
                self.add(self.at(4 - s), part_u[self.block, s - 1])
                self.add(self.at(s - 4), part_d[self.block, s - 1])
            self.landing = send(self.mine.at[self.at(4 - s)], part_u.at[self.block, s], up, RING)
            send(self.mine.at[self.at(s - 4)], part_d.at[self.block, s], down, RING, self.landing)

        def finish(self):
            assert self.step == 4
            self.landing.wait()
            rows = self.at(0)
            total = self.mine[rows].astype(F32) + part_u[self.block, 3].astype(F32) + part_d[self.block, 3].astype(F32)
            gpre[self.block, rows] = (total * slope[self.block]).astype(BF)

    class PlaneGather:
        def __init__(self, own, full):
            self.own, self.full = own, full

        def at(self, shift):
            return self.full.at[rows_of(wrap(gz + shift), ROWS)]

        def start(self):
            self.to_z = send(self.own, self.at(0), zp, PLANE)
            self.to_x = Landing()
            self.spread(self.own, 0)

        def forward(self):
            self.to_z.wait()
            self.spread(self.at(4), 4)
            self.ready = True

        def spread(self, src, shift):
            for peer in xs:
                send(src, self.at(shift), peer, PLANE, self.to_x)

        def complete(self):
            assert self.ready
            self.to_x.wait()

    class ChipReduce:
        def __init__(self, halves, compute, store):
            self.halves, self.compute, self.store = halves, compute, store

        def start(self):
            self.compute()
            self.swap = Landing()
            for p, s, _, _ in self.halves:
                send(p.at[1 - core], s, sib, CORE, self.swap)

        def total(self, h, k):
            p, s, _, _ = self.halves[h]
            return p[core, k].astype(F32) + s[k].astype(F32)

        def put(self, h, k, value):
            self.halves[h][0][core, k] = value.astype(BF)

        def chips(self):
            self.swap.wait()
            far, right, left = (lax.rem(chip + i, 4) for i in (2, 1, 3))
            (pa, _, fa, la), (pb, _, fb, lb) = self.halves
            self.put(0, far, self.total(0, far))
            self.far = send(pa.at[core, far], fa, chip_r, CHIP)
            self.put(1, far, self.total(1, far))
            send(pb.at[core, far], fb, chip_l, CHIP, self.far)
            self.put(1, right, self.total(1, right))
            self.near = send(pb.at[core, right], lb.at[0], chip_r, CHIP)
            self.put(0, left, self.total(0, left))
            send(pa.at[core, left], la.at[1], chip_l, CHIP, self.near)

        def fwd(self):
            right, left = (lax.rem(chip + i, 4) for i in (1, 3))
            (pa, _, fa, la), (pb, _, fb, lb) = self.halves
            self.far.wait()
            self.put(0, right, self.total(0, right) + fa[...].astype(F32))
            send(pa.at[core, right], la.at[0], chip_r, CHIP, self.near)
            self.put(1, left, self.total(1, left) + fb[...].astype(F32))
            send(pb.at[core, left], lb.at[1], chip_l, CHIP, self.near)

        def finish(self):
            self.near.wait()
            for h in (0, 1):
                last = self.halves[h][3]
                self.store(h, (self.total(h, chip) + last[0].astype(F32) + last[1].astype(F32)).astype(BF))

    def gelu():
        def body(i, carry):
            r = pl.ds(pl.multiple_of(i * 16, 16), 16)
            for b in range(4):
                cols = slice(b * DM, b * DM + DM)
                v = pre[r, cols].astype(F32)
                cdf = 0.5 * (1.0 + lax.erf(v * 0.7071067811865476))
                pdf = jnp.exp(-0.5 * v * v) * 0.3989422804014327
                act[rows_of(gy, ROWS, i * 16, 16), cols] = (v * cdf).astype(BF)
                slope[b, r] = cdf + v * pdf
            return carry

        lax.fori_loop(0, ROWS // 16, body, 0)

    def tn():
        pn.complete()
        normed_t[...] = normed[...].T

    def grad_down():
        ga.complete()
        pg.complete()

        def body(k, carry):
            cols = pl.ds(pl.multiple_of(k * DM, DM), DM)
            product = dot_ta(act[:, cols], grads[...]).astype(BF)
            for c in (0, 1):
                for h in (0, 1):
                    at = 192 * c + 96 * h
                    d_part[h, c, k] = product[at : at + 96]
            return carry

        lax.fori_loop(0, 4, body, 0)

    def split(product, target):
        for g in range(N):
            target[g % 2, g // 2] = product[48 * g : 48 * g + 48]

    def grad_qkv():
        gq.complete()
        split(dot(normed_t[...], qkv[:, 0:QA]).astype(BF), qa_part)
        split(dot(normed_t[...], qkv[:, QA:QW]).astype(BF), qb_part)

    def grad_up(b):
        def run():
            gp[b].complete()
            product = dot(normed_t[...], gpre[b]).astype(BF)
            split(product[:, 0:WIDE], uw_part.at[b])
            split(product[:, WIDE:DM], un_part.at[b])

        return run

    def input_qkv():
        gq.complete()
        wq.complete()

        def body(i, carry):
            r = pl.ds(pl.multiple_of(i * 256, 256), 256)
            summed[r] = dot_bt(qkv[r], w_qkv[...])
            return carry

        lax.fori_loop(0, 2, body, 0)

    plane = {}

    def input_up(b):
        gp[b].complete()
        wu.complete()

        def body(i, carry):
            r = pl.ds(pl.multiple_of(i * 256, 256), 256)
            total = summed[r] + dot_bt(gpre[b, r], w_up[:, b * DM : b * DM + DM])
            if b < 3:
                summed[r] = total
            else:
                outgoing[r] = total.astype(BF)
            return carry

        lax.fori_loop(0, 2, body, 0)

    def plane_start():
        plane["x"] = Landing()
        for d in (1, 2, 3):
            for z in (0, 1):
                rows = rows_of(z * 4 + x_index(d), ROWS)
                send(outgoing.at[rows], in_x.at[d - 1, z], xs[d - 1], PLANE, plane["x"])

    def plane_total(z):
        total = outgoing[rows_of(z * 4 + x, ROWS)].astype(F32)
        for d in range(3):
            total = total + in_x[d, z].astype(F32)
        return total

    def plane_forward():
        plane["x"].wait()
        rows = rows_of((1 - z_lo) * 4 + x, ROWS)
        outgoing[rows] = plane_total(1 - z_lo).astype(BF)
        plane["z"] = send(outgoing.at[rows], in_z, zp, PLANE)

    def plane_finish():
        plane["z"].wait()
        gi_out[...] = (plane_total(z_lo) + in_z[...].astype(F32)).astype(BF)

    def store_down(h, value):
        gwd_out[96 * h : 96 * h + 96] = value

    def store_qkv(h, value):
        cols = slice(0, QA) if h == 0 else slice(QA, QW)
        gwq_out[:, cols] = value

    def store_up(b):
        def store(h, value):
            at = b * DM + (WIDE if narrow(b) == h else 0)
            gwu_out[:, at : at + value.shape[1]] = value

        return store

    def narrow(b):
        return 1 - b % 2

    def up_halves(b):
        halves = [(uw_part.at[b], uw_sib.at[b], uw_first.at[b], uw_last.at[b]),
                  (un_part.at[b], un_sib.at[b], un_first.at[b], un_last.at[b])]
        return halves if b % 2 == 0 else halves[::-1]

    wd = ChipGather(wd_in, w_down, 192)
    wu, wq = ChipGather(wu_in, w_up, 48), ChipGather(wq_in, w_qkv, 48)
    ga, gq, gp = RingGather(act), RingGather(qkv, q_in), [BlockGather(gpre.at[b]) for b in range(4)]
    rr = [RingReduce(b) for b in range(4)]
    pg, pn = PlaneGather(g_in, grads), PlaneGather(n_in, normed)
    rd = ChipReduce([(d_part.at[h], d_sib.at[h], d_first.at[h], d_last.at[h]) for h in (0, 1)], grad_down, store_down)
    ru = [ChipReduce(up_halves(b), grad_up(b), store_up(b)) for b in range(4)]
    rq = ChipReduce([(qa_part, qa_sib, qa_first, qa_last), (qb_part, qb_sib, qb_first, qb_last)], grad_qkv, store_qkv)

    load_pre = load(p_in, pre)
    load(q_in, qkv.at[rows_of(gy, ROWS)])
    load(g_in, grads.at[rows_of(gz, ROWS)])
    load(wd_in, w_down.at[rows_of(gx, 192)])
    load(n_in, normed.at[rows_of(gz, ROWS)])
    load(wu_in, w_up.at[rows_of(gx, 48)])
    load(wq_in, w_qkv.at[rows_of(gx, 48)])
    load_pre.wait()
    gelu()
    for copy in loads[1:]:
        copy.wait()
    pl.semaphore_wait(barrier, len(peers))

    ga.go(0)
    wd.start_a()
    pn.start()
    ga.go(1)
    pg.start()
    gq.go(0)
    gq.go(1)
    wd.start_b()
    ga.go(0)
    wd.fwd()
    pn.forward()
    gq.go(0)
    pg.forward()
    wu.start_a()
    gq.go(1)
    ga.go(1)
    tn()
    wd.sh()
    wu.start_b()
    gq.go(0)
    gq.go(1)
    wd.far()
    ga.go(0)
    rr[0].start()
    rr[1].start()
    wq.start_a()
    wu.fwd()
    rr[3].start()
    rr[2].start()
    ga.go(1)
    gq.go(0)
    gq.go(1)
    wu.sh()
    rr[0].go()
    rr[2].go()
    wq.start_b()
    wq.fwd()
    ga.go(0)
    ga.go(1)
    rq.start()
    wu.far()
    rr[0].go()
    rr[1].go()
    rr[2].go()
    rq.chips()
    wq.sh()
    rr[3].go()
    rd.start()
    rr[0].go()
    wq.far()
    rr[1].go()
    rr[2].go()
    rd.chips()
    rq.fwd()
    rr[3].go()
    rr[0].finish()
    gp[0].start()
    input_qkv()
    rr[1].go()
    rr[2].finish()
    gp[2].start()
    rr[3].go()
    gp[0].go()
    rr[1].finish()
    gp[1].start()
    rd.fwd()
    gp[2].go()
    rr[3].finish()
    gp[3].start()
    gp[0].go()
    gp[1].go()
    gp[2].go()
    rq.finish()
    gp[3].go()
    gp[0].go()
    gp[1].go()
    gp[2].go()
    rd.finish()
    gp[3].go()
    ru[0].start()
    input_up(0)
    gp[1].go()
    ru[2].start()
    ru[0].chips()
    gp[3].go()
    ru[2].chips()
    ru[1].start()
    input_up(1)
    input_up(2)
    input_up(3)
    plane_start()
    ru[0].fwd()
    ru[1].chips()
    ru[3].start()
    ru[2].fwd()
    ru[3].chips()
    ru[0].finish()
    ru[1].fwd()
    plane_forward()
    ru[2].finish()
    ru[3].fwd()
    ru[1].finish()
    plane_finish()
    ru[3].finish()
    assert len(landings) == COPIES
    for link in range(LINKS):
        wait_bytes(sent[link], send_sems.at[link])


def hand_over(*refs):
    for result, out in zip(refs[:4], refs[4:]):
        out[...] = result[...]


def reduce_scratch(rows, width, *lead):
    return [
        pltpu.VMEM(lead + (2, 4, rows, width), BF),
        pltpu.VMEM(lead + (4, rows, width), BF),
        pltpu.VMEM(lead + (rows, width), BF),
        pltpu.VMEM(lead + (2, rows, width), BF),
    ]


def shards(normed, grad_out, grad_qkv_out, pre_act, w_qkv, w_up, w_down):
    ins, outs = (normed, grad_out, grad_qkv_out, pre_act, w_qkv, w_up, w_down), (normed, w_qkv, w_up, w_down)
    results = pl.pallas_call(
        kernel,
        out_shape=[pltpu.VMEM(o.shape, BF) for o in outs],
        in_specs=[pl.BlockSpec(memory_space=pltpu.HBM)] * 7,
        out_specs=[pl.BlockSpec(memory_space=pltpu.VMEM)] * 4,
        scratch_shapes=[
            pltpu.VMEM((N * ROWS, DM), BF),
            pltpu.VMEM((DM, N * ROWS), BF),
            pltpu.VMEM((N * ROWS, DM), BF),
            pltpu.VMEM((N * ROWS, QW), BF),
            pltpu.VMEM((N * ROWS, FW), BF),
            pltpu.VMEM((4, ROWS, DM), F32),
            pltpu.VMEM((FW, DM), BF),
            pltpu.VMEM((DM, FW), BF),
            pltpu.VMEM((DM, QW), BF),
            pltpu.VMEM((4, N * ROWS, DM), BF),
            pltpu.VMEM((4, 4, ROWS, DM), BF),
            pltpu.VMEM((4, 4, ROWS, DM), BF),
            pltpu.VMEM((4, N * ROWS, DM), BF),
            pltpu.VMEM((N * ROWS, DM), F32),
            pltpu.VMEM((N * ROWS, DM), BF),
            pltpu.VMEM((3, 2, ROWS, DM), BF),
            pltpu.VMEM((ROWS, DM), BF),
            *reduce_scratch(96, DM, 2),
            *reduce_scratch(48, WIDE, 4),
            *reduce_scratch(48, DM - WIDE, 4),
            *reduce_scratch(48, QA),
            *reduce_scratch(48, QB),
            pltpu.VMEM((ROWS, FW), BF),
            pltpu.VMEM((24 << 10, 128), BF),
            pltpu.SemaphoreType.DMA((LINKS,)),
            pltpu.SemaphoreType.DMA((COPIES,)),
            pltpu.SemaphoreType.DMA((7,)),
        ],
        compiler_params=pltpu.CompilerParams(
            collective_id=0, has_side_effects=True, vmem_limit_bytes=48 << 20
        ),
    )(*[pltpu.with_memory_space_constraint(a, pltpu.HBM) for a in ins])
    return pl.pallas_call(
        hand_over,
        out_shape=[jax.ShapeDtypeStruct(o.shape, BF) for o in outs],
        in_specs=[pl.BlockSpec(memory_space=pltpu.VMEM)] * 4,
        out_specs=[pl.BlockSpec(memory_space=pltpu.VMEM)] * 4,
        compiler_params=pltpu.CompilerParams(vmem_limit_bytes=4 << 20),
    )(*[pltpu.with_memory_space_constraint(r, pltpu.VMEM) for r in results])


def solution(mesh):
    rows, tall = P(("gx", "gz"), "gy"), P(("gx", "gy"), "gz")
    block, flat = P(("gy", "gx"), "gz"), P(("gz", "gx"), "gy")
    return jax.shard_map(
        shards,
        mesh=mesh,
        in_specs=(rows, rows, tall, tall, block, block, flat),
        out_specs=(rows, block, block, flat),
        check_vma=False,
    )
```

```python
import math

import jax
import jax.numpy as jnp
from jax import lax
from jax.experimental import pallas as pl
from jax.experimental.pallas import tpu as pltpu
from jax.sharding import PartitionSpec as P

MESH = pl.DeviceIdType.MESH
BF = jnp.bfloat16
F32 = jnp.float32
N = 8
ROWS = 64
HALF = 32
DM = 384
QW = 1152
FW = 1536
QA = 640
QB = 512
WIDE = 256
COPIES = 84
RING, CHIP, CORE, PLANE = range(4)
LINKS = 4


def dot_bt(a, b):
    return lax.dot_general(a, b, (((1,), (1,)), ((), ())), preferred_element_type=F32)


def dot_ta(a, b):
    return lax.dot_general(a, b, (((0,), (0,)), ((), ())), preferred_element_type=F32)


def dot(a, b):
    return jnp.dot(a, b, preferred_element_type=F32)


def wrap(i):
    return lax.rem(i + 2 * N, N)


def rows_of(slot, size, start=0, count=None):
    count = size if count is None else count
    return pl.ds(pl.multiple_of(slot * size + start, 16), count)


def kernel(
    n_in, g_in, q_in, p_in, wq_in, wu_in, wd_in,
    gi_out, gwq_out, gwu_out, gwd_out,
    normed, normed_t, grads, qkv, act, slope, w_down, w_up, w_qkv,
    part, part_u, part_d, gpre, summed, outgoing, in_x, in_z,
    d_part, d_sib, d_first, d_last,
    uw_part, uw_sib, uw_first, uw_last,
    un_part, un_sib, un_first, un_last,
    qa_part, qa_sib, qa_first, qa_last,
    qb_part, qb_sib, qb_first, qb_last,
    pre, size_ref, send_sems, recv_sems, load_sems,
):
    gx, gy, gz = lax.axis_index("gx"), lax.axis_index("gy"), lax.axis_index("gz")
    core = lax.rem(gx, 2)
    chip = gx // 2
    z_lo, x = gz // 4, lax.rem(gz, 4)

    sib = (gx + 1 - 2 * core, gy, gz)
    chip_r, chip_l = (wrap(gx + 2), gy, gz), (wrap(gx - 2), gy, gz)
    up, down = (gx, wrap(gy + 1), gz), (gx, wrap(gy - 1), gz)
    zp = (gx, gy, wrap(gz + 4))

    def x_index(shift):
        return lax.rem(x + shift, 4)

    xs = [(gx, gy, z_lo * 4 + x_index(d)) for d in (1, 2, 3)]

    barrier = pltpu.get_barrier_semaphore()
    peers = [sib, chip_r, chip_l, up, down, zp] + xs
    for peer in peers:
        pl.semaphore_signal(barrier, inc=1, device_id=peer, device_id_type=MESH)

    loads = []

    def load(src, dst):
        copy = pltpu.make_async_copy(src, dst, load_sems.at[min(len(loads), 1)])
        copy.start()
        loads.append(copy)
        return copy

    sent = [0] * LINKS
    landings = []

    def wait_bytes(count, sem):
        piece = size_ref.at[pl.ds(0, count // 256)]
        pltpu.make_async_copy(piece, piece, sem).wait()

    class Landing:
        def __init__(self):
            self.sem = recv_sems.at[len(landings)]
            self.bytes = 0
            self.done = False
            landings.append(self)

        def wait(self):
            if not self.done:
                wait_bytes(self.bytes, self.sem)
            self.done = True

    def send(src, dst, peer, link, landing=None):
        landing = Landing() if landing is None else landing
        assert not landing.done
        pltpu.make_async_remote_copy(
            src_ref=src, dst_ref=dst, send_sem=send_sems.at[link], recv_sem=landing.sem,
            device_id=peer, device_id_type=MESH,
        ).start()
        size = 2 * math.prod(src.shape)
        landing.bytes += size
        sent[link] += size
        return landing

    def wait_all(copies):
        for copy in copies:
            copy.wait()

    class ChipGather:
        def __init__(self, own, full, size):
            self.own, self.full, self.size = own, full, size
            self.to_sib = Landing()
            self.count = 0

        def half_at(self, h):
            if self.size % 32 == 0:
                return (pl.ds(h * self.size // 2, self.size // 2),)
            width = self.full.shape[1] // 256 * 128
            return (slice(None), pl.ds(0, width) if h == 0 else pl.ds(width, self.full.shape[1] - width))

        def at(self, shift):
            return self.full.at[rows_of(wrap(gx + shift), self.size)]

        def half(self, shift, h):
            return self.at(shift).at[self.half_at(h)]

        def share(self, src, dst):
            self.count += 1
            send(src, dst, sib, CORE, self.to_sib)

        def start_a(self):
            self.a = send(self.own.at[self.half_at(0)], self.half(0, 0), chip_r, CHIP)
            send(self.own.at[self.half_at(1)], self.half(0, 1), chip_l, CHIP, self.a)
            self.share(self.own, self.at(0))

        def start_b(self):
            self.b = send(self.own.at[self.half_at(1)], self.half(0, 1), chip_r, CHIP)
            send(self.own.at[self.half_at(0)], self.half(0, 0), chip_l, CHIP, self.b)

        def fwd(self):
            self.a.wait()
            self.c = send(self.half(-2, 0), self.half(-2, 0), chip_r, CHIP)
            send(self.half(2, 1), self.half(2, 1), chip_l, CHIP, self.c)

        def sh(self):
            self.b.wait()
            self.share(self.at(-2), self.at(-2))
            self.share(self.at(2), self.at(2))

        def far(self):
            self.c.wait()
            self.share(self.half(4, 0), self.half(4, 0))
            self.share(self.half(4, 1), self.half(4, 1))

        def complete(self):
            assert self.count == 5
            self.to_sib.wait()

    class RingGather:
        def __init__(self, full, own=None):
            self.full, self.own = full, own
            self.chain = {}
            self.hops = {}

        def at(self, shift, h):
            return self.full.at[rows_of(wrap(gy + shift), ROWS, HALF * h, HALF)]

        def go(self, h):
            s = self.hops.get(h, 0)
            self.hops[h] = s + 1
            if s > 0:
                self.chain[h].wait()
            self.chain[h] = Landing()
            for d, peer in ((0, up), (1, down)):
                if s < 3 or d == h:
                    here = self.at(s if d else -s, h)
                    src = self.own.at[pl.ds(HALF * h, HALF)] if s == 0 and self.own is not None else here
                    send(src, here, peer, RING, self.chain[h])

        def complete(self):
            assert self.hops == {0: 4, 1: 4}
            for h in (0, 1):
                self.chain[h].wait()

    class BlockGather:
        def __init__(self, full):
            self.full = full

        def at(self, shift, start=0, count=ROWS):
            return self.full.at[rows_of(wrap(gy + shift), ROWS, start, count)]

        def start(self):
            self.step = 0
            self.go()

        def go(self):
            s = self.step
            self.step += 1
            if s > 0:
                self.landing.wait()
            self.landing = Landing()
            src = self.at(-s, 0, ROWS if s < 3 else HALF)
            send(src, src, up, RING, self.landing)
            src = self.at(s) if s < 3 else self.at(3, HALF, HALF)
            send(src, src, down, RING, self.landing)

        def complete(self):
            assert self.step == 4
            self.landing.wait()

    class RingReduce:
        def __init__(self, block):
            self.block = block
            self.mine = part.at[self.block]

        def at(self, shift, start=0, count=ROWS):
            return rows_of(wrap(gy + shift), ROWS, start, count)

        def start(self):
            pg.complete()
            wd.complete()
            rows = rows_of(self.block, DM)

            def body(i, carry):
                r = pl.ds(pl.multiple_of(i * 256, 256), 256)
                self.mine[r] = dot_bt(grads[r], w_down[rows]).astype(BF)
                return carry

            lax.fori_loop(0, 2, body, 0)
            self.step = 1
            half = self.at(4, 0, HALF), self.at(4, HALF, HALF)
            self.landing = send(self.mine.at[half[0]], part_u.at[self.block, 0, pl.ds(0, HALF)], up, RING)
            send(self.mine.at[half[1]], part_d.at[self.block, 0, pl.ds(HALF, HALF)], down, RING, self.landing)

        def add(self, rows, other):
            self.mine[rows] = (self.mine[rows].astype(F32) + other.astype(F32)).astype(BF)

        def go(self):
            s = self.step
            self.step += 1
            self.landing.wait()
            if s == 1:
                self.add(self.at(3, 0, HALF), part_u[self.block, 0, 0:HALF])
                self.add(self.at(-3, HALF, HALF), part_d[self.block, 0, HALF:ROWS])
            else:
                self.add(self.at(4 - s), part_u[self.block, s - 1])
                self.add(self.at(s - 4), part_d[self.block, s - 1])
            self.landing = send(self.mine.at[self.at(4 - s)], part_u.at[self.block, s], up, RING)
            send(self.mine.at[self.at(s - 4)], part_d.at[self.block, s], down, RING, self.landing)

        def finish(self):
            assert self.step == 4
            self.landing.wait()
            rows = self.at(0)
            total = self.mine[rows].astype(F32) + part_u[self.block, 3].astype(F32) + part_d[self.block, 3].astype(F32)
            gpre[self.block, rows] = (total * slope[self.block]).astype(BF)

    class PlaneGather:
        def __init__(self, own, full):
            self.own, self.full = own, full

        def at(self, shift):
            return self.full.at[rows_of(wrap(gz + shift), ROWS)]

        def start(self):
            self.to_z = send(self.own, self.at(0), zp, PLANE)
            self.to_x = Landing()
            self.spread(self.own, 0)

        def forward(self):
            self.to_z.wait()
            self.spread(self.at(4), 4)
            self.ready = True

        def spread(self, src, shift):
            for peer in xs:
                send(src, self.at(shift), peer, PLANE, self.to_x)

        def complete(self):
            assert self.ready
            self.to_x.wait()

    class ChipReduce:
        def __init__(self, halves, compute, store):
            self.halves, self.compute, self.store = halves, compute, store

        def start(self):
            self.compute()
            self.swap = Landing()
            for p, s, _, _ in self.halves:
                send(p.at[1 - core], s, sib, CORE, self.swap)

        def total(self, h, k):
            p, s, _, _ = self.halves[h]
            return p[core, k].astype(F32) + s[k].astype(F32)

        def put(self, h, k, value):
            self.halves[h][0][core, k] = value.astype(BF)

        def chips(self):
            self.swap.wait()
            far, right, left = (lax.rem(chip + i, 4) for i in (2, 1, 3))
            (pa, _, fa, la), (pb, _, fb, lb) = self.halves
            self.put(0, far, self.total(0, far))
            self.far = send(pa.at[core, far], fa, chip_r, CHIP)
            self.put(1, far, self.total(1, far))
            send(pb.at[core, far], fb, chip_l, CHIP, self.far)
            self.put(1, right, self.total(1, right))
            self.near = send(pb.at[core, right], lb.at[0], chip_r, CHIP)
            self.put(0, left, self.total(0, left))
            send(pa.at[core, left], la.at[1], chip_l, CHIP, self.near)

        def fwd(self):
            right, left = (lax.rem(chip + i, 4) for i in (1, 3))
            (pa, _, fa, la), (pb, _, fb, lb) = self.halves
            self.far.wait()
            self.put(0, right, self.total(0, right) + fa[...].astype(F32))
            send(pa.at[core, right], la.at[0], chip_r, CHIP, self.near)
            self.put(1, left, self.total(1, left) + fb[...].astype(F32))
            send(pb.at[core, left], lb.at[1], chip_l, CHIP, self.near)

        def finish(self):
            self.near.wait()
            for h in (0, 1):
                last = self.halves[h][3]
                self.store(h, (self.total(h, chip) + last[0].astype(F32) + last[1].astype(F32)).astype(BF))

    def gelu():
        def body(i, carry):
            r = pl.ds(pl.multiple_of(i * 16, 16), 16)
            for b in range(4):
                cols = slice(b * DM, b * DM + DM)
                v = pre[r, cols].astype(F32)
                cdf = 0.5 * (1.0 + lax.erf(v * 0.7071067811865476))
                pdf = jnp.exp(-0.5 * v * v) * 0.3989422804014327
                act[rows_of(gy, ROWS, i * 16, 16), cols] = (v * cdf).astype(BF)
                slope[b, r] = cdf + v * pdf
            return carry

        lax.fori_loop(0, ROWS // 16, body, 0)

    def tn():
        pn.complete()
        normed_t[...] = normed[...].T

    def grad_down():
        ga.complete()
        pg.complete()

        def body(k, carry):
            cols = pl.ds(pl.multiple_of(k * DM, DM), DM)
            product = dot_ta(act[:, cols], grads[...]).astype(BF)
            for c in (0, 1):
                for h in (0, 1):
                    at = 192 * c + 96 * h
                    d_part[h, c, k] = product[at : at + 96]
            return carry

        lax.fori_loop(0, 4, body, 0)

    def split(product, target):
        for g in range(N):
            target[g % 2, g // 2] = product[48 * g : 48 * g + 48]

    def grad_qkv():
        gq.complete()
        split(dot(normed_t[...], qkv[:, 0:QA]).astype(BF), qa_part)
        split(dot(normed_t[...], qkv[:, QA:QW]).astype(BF), qb_part)

    def grad_up(b):
        def run():
            gp[b].complete()
            product = dot(normed_t[...], gpre[b]).astype(BF)
            split(product[:, 0:WIDE], uw_part.at[b])
            split(product[:, WIDE:DM], un_part.at[b])

        return run

    def input_qkv():
        gq.complete()
        wq.complete()

        def body(i, carry):
            r = pl.ds(pl.multiple_of(i * 256, 256), 256)
            summed[r] = dot_bt(qkv[r], w_qkv[...])
            return carry

        lax.fori_loop(0, 2, body, 0)

    plane = {}

    def input_up(b):
        gp[b].complete()
        wu.complete()

        def body(i, carry):
            r = pl.ds(pl.multiple_of(i * 256, 256), 256)
            total = summed[r] + dot_bt(gpre[b, r], w_up[:, b * DM : b * DM + DM])
            if b < 3:
                summed[r] = total
            else:
                outgoing[r] = total.astype(BF)
            return carry

        lax.fori_loop(0, 2, body, 0)

    def plane_start():
        plane["x"] = Landing()
        for d in (1, 2, 3):
            for z in (0, 1):
                rows = rows_of(z * 4 + x_index(d), ROWS)
                send(outgoing.at[rows], in_x.at[d - 1, z], xs[d - 1], PLANE, plane["x"])

    def plane_total(z):
        total = outgoing[rows_of(z * 4 + x, ROWS)].astype(F32)
        for d in range(3):
            total = total + in_x[d, z].astype(F32)
        return total

    def plane_forward():
        plane["x"].wait()
        rows = rows_of((1 - z_lo) * 4 + x, ROWS)
        outgoing[rows] = plane_total(1 - z_lo).astype(BF)
        plane["z"] = send(outgoing.at[rows], in_z, zp, PLANE)

    def plane_finish():
        plane["z"].wait()
        gi_out[...] = (plane_total(z_lo) + in_z[...].astype(F32)).astype(BF)

    def store_down(h, value):
        gwd_out[96 * h : 96 * h + 96] = value

    def store_qkv(h, value):
        cols = slice(0, QA) if h == 0 else slice(QA, QW)
        gwq_out[:, cols] = value

    def store_up(b):
        def store(h, value):
            at = b * DM + (WIDE if narrow(b) == h else 0)
            gwu_out[:, at : at + value.shape[1]] = value

        return store

    def narrow(b):
        return 1 - b % 2

    def up_halves(b):
        halves = [(uw_part.at[b], uw_sib.at[b], uw_first.at[b], uw_last.at[b]),
                  (un_part.at[b], un_sib.at[b], un_first.at[b], un_last.at[b])]
        return halves if b % 2 == 0 else halves[::-1]

    wd = ChipGather(wd_in, w_down, 192)
    wu, wq = ChipGather(wu_in, w_up, 48), ChipGather(wq_in, w_qkv, 48)
    ga, gq, gp = RingGather(act), RingGather(qkv, q_in), [BlockGather(gpre.at[b]) for b in range(4)]
    rr = [RingReduce(b) for b in range(4)]
    pg, pn = PlaneGather(g_in, grads), PlaneGather(n_in, normed)
    rd = ChipReduce([(d_part.at[h], d_sib.at[h], d_first.at[h], d_last.at[h]) for h in (0, 1)], grad_down, store_down)
    ru = [ChipReduce(up_halves(b), grad_up(b), store_up(b)) for b in range(4)]
    rq = ChipReduce([(qa_part, qa_sib, qa_first, qa_last), (qb_part, qb_sib, qb_first, qb_last)], grad_qkv, store_qkv)

    load_pre = load(p_in, pre)
    load(q_in, qkv.at[rows_of(gy, ROWS)])
    load(g_in, grads.at[rows_of(gz, ROWS)])
    load(wd_in, w_down.at[rows_of(gx, 192)])
    load(n_in, normed.at[rows_of(gz, ROWS)])
    load(wu_in, w_up.at[rows_of(gx, 48)])
    load(wq_in, w_qkv.at[rows_of(gx, 48)])
    load_pre.wait()
    gelu()
    pl.semaphore_wait(barrier, len(peers))

    ga.go(0)
    wd.start_a()
    pn.start()
    ga.go(1)
    pg.start()
    gq.go(0)
    gq.go(1)
    wd.start_b()
    own = (q_in, g_in, wd_in, n_in, wu_in, wq_in)
    wait_bytes(sum(2 * math.prod(ref.shape) for ref in own), load_sems.at[1])
    ga.go(0)
    wd.fwd()
    pn.forward()
    gq.go(0)
    pg.forward()
    wu.start_a()
    gq.go(1)
    ga.go(1)
    tn()
    wd.sh()
    wu.start_b()
    gq.go(0)
    gq.go(1)
    wd.far()
    ga.go(0)
    rr[0].start()
    rr[1].start()
    wq.start_a()
    wu.fwd()
    rr[3].start()
    rr[2].start()
    ga.go(1)
    gq.go(0)
    gq.go(1)
    wu.sh()
    rr[0].go()
    rr[2].go()
    wq.start_b()
    wq.fwd()
    ga.go(0)
    ga.go(1)
    rq.start()
    wu.far()
    rr[0].go()
    rr[1].go()
    rr[2].go()
    rq.chips()
    wq.sh()
    rr[3].go()
    rd.start()
    rr[0].go()
    wq.far()
    rr[1].go()
    rr[2].go()
    rd.chips()
    rq.fwd()
    rr[3].go()
    rr[0].finish()
    gp[0].start()
    input_qkv()
    rr[1].go()
    rr[2].finish()
    gp[2].start()
    rr[3].go()
    gp[0].go()
    rr[1].finish()
    gp[1].start()
    rd.fwd()
    gp[2].go()
    rr[3].finish()
    gp[3].start()
    gp[0].go()
    gp[1].go()
    gp[2].go()
    rq.finish()
    gp[3].go()
    gp[0].go()
    gp[1].go()
    gp[2].go()
    rd.finish()
    gp[3].go()
    ru[0].start()
    input_up(0)
    gp[1].go()
    ru[2].start()
    ru[0].chips()
    gp[3].go()
    ru[2].chips()
    ru[1].start()
    input_up(1)
    input_up(2)
    input_up(3)
    plane_start()
    ru[0].fwd()
    ru[1].chips()
    ru[3].start()
    ru[2].fwd()
    ru[3].chips()
    ru[0].finish()
    ru[1].fwd()
    plane_forward()
    ru[2].finish()
    ru[3].fwd()
    ru[1].finish()
    plane_finish()
    ru[3].finish()
    assert len(landings) == COPIES
    for link in range(LINKS):
        wait_bytes(sent[link], send_sems.at[link])


def hand_over(*refs):
    for result, out in zip(refs[:4], refs[4:]):
        out[...] = result[...]


def reduce_scratch(rows, width, *lead):
    return [
        pltpu.VMEM(lead + (2, 4, rows, width), BF),
        pltpu.VMEM(lead + (4, rows, width), BF),
        pltpu.VMEM(lead + (rows, width), BF),
        pltpu.VMEM(lead + (2, rows, width), BF),
    ]


def shards(normed, grad_out, grad_qkv_out, pre_act, w_qkv, w_up, w_down):
    ins, outs = (normed, grad_out, grad_qkv_out, pre_act, w_qkv, w_up, w_down), (normed, w_qkv, w_up, w_down)
    results = pl.pallas_call(
        kernel,
        out_shape=[pltpu.VMEM(o.shape, BF) for o in outs],
        in_specs=[pl.BlockSpec(memory_space=pltpu.HBM)] * 7,
        out_specs=[pl.BlockSpec(memory_space=pltpu.VMEM)] * 4,
        scratch_shapes=[
            pltpu.VMEM((N * ROWS, DM), BF),
            pltpu.VMEM((DM, N * ROWS), BF),
            pltpu.VMEM((N * ROWS, DM), BF),
            pltpu.VMEM((N * ROWS, QW), BF),
            pltpu.VMEM((N * ROWS, FW), BF),
            pltpu.VMEM((4, ROWS, DM), F32),
            pltpu.VMEM((FW, DM), BF),
            pltpu.VMEM((DM, FW), BF),
            pltpu.VMEM((DM, QW), BF),
            pltpu.VMEM((4, N * ROWS, DM), BF),
            pltpu.VMEM((4, 4, ROWS, DM), BF),
            pltpu.VMEM((4, 4, ROWS, DM), BF),
            pltpu.VMEM((4, N * ROWS, DM), BF),
            pltpu.VMEM((N * ROWS, DM), F32),
            pltpu.VMEM((N * ROWS, DM), BF),
            pltpu.VMEM((3, 2, ROWS, DM), BF),
            pltpu.VMEM((ROWS, DM), BF),
            *reduce_scratch(96, DM, 2),
            *reduce_scratch(48, WIDE, 4),
            *reduce_scratch(48, DM - WIDE, 4),
            *reduce_scratch(48, QA),
            *reduce_scratch(48, QB),
            pltpu.VMEM((ROWS, FW), BF),
            pltpu.VMEM((24 << 10, 128), BF),
            pltpu.SemaphoreType.DMA((LINKS,)),
            pltpu.SemaphoreType.DMA((COPIES,)),
            pltpu.SemaphoreType.DMA((2,)),
        ],
        compiler_params=pltpu.CompilerParams(
            collective_id=0, has_side_effects=True, vmem_limit_bytes=48 << 20
        ),
    )(*[pltpu.with_memory_space_constraint(a, pltpu.HBM) for a in ins])
    return pl.pallas_call(
        hand_over,
        out_shape=[jax.ShapeDtypeStruct(o.shape, BF) for o in outs],
        in_specs=[pl.BlockSpec(memory_space=pltpu.VMEM)] * 4,
        out_specs=[pl.BlockSpec(memory_space=pltpu.VMEM)] * 4,
        compiler_params=pltpu.CompilerParams(vmem_limit_bytes=4 << 20),
    )(*[pltpu.with_memory_space_constraint(r, pltpu.VMEM) for r in results])


def solution(mesh):
    rows, tall = P(("gx", "gz"), "gy"), P(("gx", "gy"), "gz")
    block, flat = P(("gy", "gx"), "gz"), P(("gz", "gx"), "gy")
    return jax.shard_map(
        shards,
        mesh=mesh,
        in_specs=(rows, rows, tall, tall, block, block, flat),
        out_specs=(rows, block, block, flat),
        check_vma=False,
    )
```
